256 devices in a mesh: rows: 64 (over x, z, core), cols: 4 (over y).
Axes of the slice: x: 4, y: 4, z: 8, core: 2. Of those that a mesh axis runs over, the one named last changes fastest.
Arguments:
- points: bfloat16 [128, 262144], P('cols', 'rows'), may hold values from -6 to 6
- basis: bfloat16 [4096, 64, 64], P('rows'), may hold values from -0.75 to 0.75
- leaf_transfer: bfloat16 [4096, 64, 64], P('rows'), may hold values from -0.5 to 0.5
- box_transfer: bfloat16 [512, 64, 64], P('rows'), may hold values from -0.5 to 0.5
- coarse_transfer: bfloat16 [96, 64, 64], replicated, may hold values from -0.5 to 0.5
- send_leaf: int32 [4096, 16], P('rows', 'cols'), may hold values from -1 to 63, as said below
- leaf_far: int32 [4096, 24], P('rows', 'cols'), may hold values from 0 to 255, as said below
- leaf_coupling: bfloat16 [4096, 24, 64, 64], P('rows', 'cols'), may hold values from -0.15625 to 0.15625
- send_box: int32 [4096, 8], P('rows', 'cols'), may hold values from -1 to 7, as said below
- box_far: int32 [512, 16], P('rows', 'cols'), may hold values from 0 to 127, as said below
- box_coupling: bfloat16 [512, 16, 64, 64], P('rows', 'cols'), may hold values from -0.09375 to 0.09375
- coarse_far: int32 [112, 8], P(None, 'cols'), may hold values from 0 to 111, as said below
- coarse_coupling: bfloat16 [112, 8, 64, 64], P(None, 'cols'), may hold values from -0.0625 to 0.0625
- near_index: int32 [4096, 8], P('rows'), may hold values from 0 to 4095, as said below
- near_block: bfloat16 [4096, 8, 64, 64], P('rows'), may hold values from -0.25 to 0.25
Outputs:
- product: bfloat16 [128, 262144], P('cols', 'rows')
The draws below stay inside these ranges and needn't reach their ends.
Inputs may be any that keep to these rules, and one draw needn't show every extreme that they name: `send_leaf`: row p * 64 + d, columns q * 4 to q * 4 + 3: distinct leaf numbers within device p, live ones first and -1 after them; every such group has at least one live entry, and in every draw one device d receives a full 4 from every device p in some share. `leaf_far`: an entry in columns q * 6 onward of a leaf on device d is p * 4 + s with s a live position of row p * 64 + d, share q, of send_leaf. `send_box`: row p * 64 + d, columns q * 2 to q * 2 + 1: distinct box numbers within device p, live ones first and -1 after them; every such group has at least one live entry, and in every draw one device d receives a full 2 from every device p in some share. `box_far`: an entry in columns q * 4 onward of a box on device d is p * 2 + s with s a live position of row p * 64 + d, share q, of send_box. `coarse_far`: entries of node i name nodes of the same level as i (levels: indices below 16, below 48, the rest), never i itself; entries may repeat. `near_index`: entry 0 of leaf l is l itself; every entry names a leaf on the device of l or on a device next to it along rows.
All inputs are finite; a program needn't handle non-finite values.
Results may differ from the reference program's by a relative error of at most 0.0052.
Values may be sent and summed in bfloat16 or wider, within the bound.
A program may use at most 128 MiB of HBM per device.

```python
import jax
import jax.numpy as jnp
from jax import lax

B = 64
R = 64
NVEC = 128
LEAF_DEV = 64
BOX_DEV = 8
NEAR = 8
FCOL0 = 6
FCOL1 = 4
SLOT0 = 4
SLOT1 = 2
LEAVES = 4096
POINTS = 262144
BOXES = 512
CN = 112
CT = 96
FAR0 = 24
FAR1 = 16
FARC = 8
N_ROWS = 64
N_COLS = 4


def exchange_plan(key, node_count, slot_count, list_count, level_tag):
    key = jax.random.fold_in(key, level_tag)
    keys = jax.random.split(key, 5)
    device_count = N_ROWS
    share_count = N_COLS
    live = jax.random.randint(keys[0], (share_count, device_count, device_count), 1, slot_count + 1)
    full_target = jax.random.randint(keys[1], (share_count,), 0, device_count)
    targets = jnp.arange(device_count)
    live = jnp.where(targets[None, None, :] == full_target[:, None, None], slot_count, live)
    scores = jax.random.randint(keys[2], (share_count, device_count, device_count, node_count), 0, 4096) * node_count + jnp.arange(node_count)
    chosen = jnp.argsort(scores, axis=-1, stable=True)[..., :slot_count]
    used = jnp.arange(slot_count)[None, None, None, :] < live[..., None]
    sent = jnp.where(used, chosen, -1).astype(jnp.int32)
    sent = sent.transpose(1, 2, 0, 3).reshape(device_count * device_count, share_count * slot_count)
    peers = jax.random.randint(keys[3], (device_count, node_count, share_count, list_count), 0, device_count)
    picks = jax.random.randint(keys[4], (device_count, node_count, share_count, list_count), 0, 1 << 20)
    share_ids = jnp.arange(share_count)[None, None, :, None]
    receiver_ids = jnp.arange(device_count)[:, None, None, None]
    limits = live[share_ids, peers, receiver_ids]
    slots = (peers * slot_count + picks % limits).astype(jnp.int32)
    return (sent, slots.reshape(device_count * node_count, share_count * list_count))


def draw_send_leaf(key, part):
    sent, slots = exchange_plan(key, LEAF_DEV, SLOT0, FCOL0, 11)
    return sent


def draw_leaf_far(key, part):
    sent, slots = exchange_plan(key, LEAF_DEV, SLOT0, FCOL0, 11)
    return slots


def draw_send_box(key, part):
    sent, slots = exchange_plan(key, BOX_DEV, SLOT1, FCOL1, 12)
    return sent


def draw_box_far(key, part):
    sent, slots = exchange_plan(key, BOX_DEV, SLOT1, FCOL1, 12)
    return slots


def draw_coarse_far(key, part):
    key = jax.random.fold_in(key, 31)
    device_count = N_ROWS
    heap = jnp.arange(CN) + device_count // 4
    level_start = jnp.where(heap >= device_count, device_count, jnp.where(heap >= device_count // 2, device_count // 2, device_count // 4))
    offsets = jax.random.randint(key, (CN, FARC), 0, 1 << 20) % (level_start[:, None] - 1) + 1
    partner = level_start[:, None] + (heap[:, None] - level_start[:, None] + offsets) % level_start[:, None]
    return (partner - device_count // 4).astype(jnp.int32)


def draw_near_index(key, part):
    key = jax.random.fold_in(key, 21)
    keys = jax.random.split(key, 2)
    owners = jnp.arange(LEAVES)
    device = owners // LEAF_DEV
    shifts = jax.random.randint(keys[0], (LEAVES, NEAR), -1, 2)
    partner_device = jnp.clip(device[:, None] + shifts, 0, N_ROWS - 1)
    partner_leaf = jax.random.randint(keys[1], (LEAVES, NEAR), 0, LEAF_DEV)
    chosen = partner_device * LEAF_DEV + partner_leaf
    column = jnp.arange(NEAR)[None, :]
    return jnp.where(column == 0, owners[:, None], chosen).astype(jnp.int32)


def steps_of(rng, extent, pieces, smallest, top_value):
    gain = 1.0
    for dim, shards_of in pieces:
        heights = jax.random.uniform(jax.random.fold_in(jax.random.fold_in(rng, 6), dim), (shards_of,), jnp.float32, smallest / len(pieces), top_value / len(pieces))
        gain = gain * jnp.repeat(jnp.exp(heights), extent[dim] // shards_of).reshape((-1,) + (1,) * (len(extent) - 1 - dim))
    return gain


def bell_draw(rng, extent, width, bound, cuts=(), held_as=jnp.bfloat16):
    gain = steps_of(rng, extent, cuts, -0.22, 0.18) if cuts else 1.0
    drawn = jax.random.normal(rng, extent, jnp.float32) * width * gain
    return jnp.minimum(jnp.maximum(drawn, -bound), bound).astype(held_as)


def setup_inputs(seed: int = 0) -> dict:
    splits = jax.random.split(jax.random.key(seed), 16)
    return {
        "points": bell_draw(splits[0], (NVEC, POINTS), 1.0, 6.0, ((0, 4), (1, 64))),
        "basis": bell_draw(splits[1], (LEAVES, B, R), B ** -0.5, 0.75, ((0, 64),)),
        "leaf_transfer": bell_draw(splits[2], (LEAVES, R, R), (2 * R) ** -0.5, 0.5, ((0, 64),)),
        "box_transfer": bell_draw(splits[3], (BOXES, R, R), (2 * R) ** -0.5, 0.5, ((0, 64),)),
        "coarse_transfer": bell_draw(splits[4], (CT, R, R), (2 * R) ** -0.5, 0.5),
        "send_leaf": draw_send_leaf(jax.random.fold_in(splits[15], 71), 0),
        "leaf_far": draw_leaf_far(jax.random.fold_in(splits[15], 71), 0),
        "leaf_coupling": bell_draw(splits[7], (LEAVES, FAR0, R, R), (FAR0 * R) ** -0.5, 0.15625, ((0, 64), (1, 4))),
        "send_box": draw_send_box(jax.random.fold_in(splits[15], 71), 0),
        "box_far": draw_box_far(jax.random.fold_in(splits[15], 71), 0),
        "box_coupling": bell_draw(splits[10], (BOXES, FAR1, R, R), (4 * FAR1 * R) ** -0.5, 0.09375, ((0, 64), (1, 4))),
        "coarse_far": draw_coarse_far(jax.random.fold_in(splits[15], 71), 0),
        "coarse_coupling": bell_draw(splits[12], (CN, FARC, R, R), (16 * FARC * R) ** -0.5, 0.0625, ((1, 4),)),
        "near_index": draw_near_index(jax.random.fold_in(splits[15], 71), 0),
        "near_block": bell_draw(splits[14], (LEAVES, NEAR, B, B), (NEAR * B) ** -0.5, 0.25, ((0, 64),)),
    }


HIGHEST = lax.Precision.HIGHEST


def widen(array):
    return array.astype(jnp.float32)


def lower_field(transfer, parent_field):
    return jnp.einsum('krs,kvs->kvr', widen(transfer), parent_field, precision=HIGHEST)


def reference(points, basis, leaf_transfer, box_transfer, coarse_transfer, send_leaf, leaf_far, leaf_coupling, send_box, box_far, box_coupling, coarse_far, coarse_coupling, near_index, near_block):
    row_count = N_ROWS
    half_rows = row_count // 2
    quarter_rows = row_count // 4
    point_blocks = points.reshape(NVEC, LEAVES, B)
    coef_leaf = jnp.einsum('vlb,lbr->lvr', widen(point_blocks), widen(basis), precision=HIGHEST).astype(jnp.bfloat16)
    coef_box = jnp.einsum('kjvr,kjrs->kvs', widen(coef_leaf.reshape(BOXES, 8, NVEC, R)), widen(leaf_transfer.reshape(BOXES, 8, R, R)), precision=HIGHEST).astype(jnp.bfloat16)
    coef_root = jnp.einsum('dkvr,dkrs->dvs', widen(coef_box.reshape(row_count, BOX_DEV, NVEC, R)), widen(box_transfer.reshape(row_count, BOX_DEV, R, R)), precision=HIGHEST).astype(jnp.bfloat16)
    coef_mid = jnp.einsum('jtvr,jtrs->jvs', widen(coef_root.reshape(half_rows, 2, NVEC, R)), widen(coarse_transfer[half_rows:].reshape(half_rows, 2, R, R)), precision=HIGHEST).astype(jnp.bfloat16)
    coef_top = jnp.einsum('jtvr,jtrs->jvs', widen(coef_mid.reshape(quarter_rows, 2, NVEC, R)), widen(coarse_transfer[:half_rows].reshape(quarter_rows, 2, R, R)), precision=HIGHEST).astype(jnp.bfloat16)
    coef_coarse = jnp.concatenate([coef_top, coef_mid, coef_root], axis=0)
    far_coarse = jnp.einsum('ifrs,ifvs->ivr', widen(coarse_coupling), widen(coef_coarse[coarse_far]), precision=HIGHEST)
    field_top = far_coarse[:quarter_rows]
    field_mid = lower_field(coarse_transfer[:half_rows], jnp.repeat(field_top, 2, axis=0)) + far_coarse[quarter_rows:3 * quarter_rows]
    field_root = lower_field(coarse_transfer[half_rows:], jnp.repeat(field_mid, 2, axis=0)) + far_coarse[3 * quarter_rows:]
    share_leaf = (jnp.arange(FAR0) // FCOL0).astype(jnp.int32)
    share_box = (jnp.arange(FAR1) // FCOL1).astype(jnp.int32)

    def one_device(device):
        leaf_start = (device * LEAF_DEV).astype(jnp.int32)
        box_start = (device * BOX_DEV).astype(jnp.int32)
        leaf_slots = lax.dynamic_slice_in_dim(leaf_far, leaf_start, LEAF_DEV, 0)
        leaf_peers = leaf_slots // SLOT0
        leaf_nodes = send_leaf[leaf_peers * row_count + device, share_leaf[None, :] * SLOT0 + leaf_slots % SLOT0]
        partner_leaf = leaf_peers * LEAF_DEV + leaf_nodes
        box_slots = lax.dynamic_slice_in_dim(box_far, box_start, BOX_DEV, 0)
        box_peers = box_slots // SLOT1
        box_nodes = send_box[box_peers * row_count + device, share_box[None, :] * SLOT1 + box_slots % SLOT1]
        partner_box = box_peers * BOX_DEV + box_nodes
        leaf_terms = lax.dynamic_slice_in_dim(leaf_coupling, leaf_start, LEAF_DEV, 0)
        box_terms = lax.dynamic_slice_in_dim(box_coupling, box_start, BOX_DEV, 0)
        far_leaf = jnp.einsum('lfrs,lfvs->lvr', widen(leaf_terms), widen(coef_leaf[partner_leaf]), precision=HIGHEST)
        far_box = jnp.einsum('kfrs,kfvs->kvr', widen(box_terms), widen(coef_box[partner_box]), precision=HIGHEST)
        box_matrices = lax.dynamic_slice_in_dim(box_transfer, box_start, BOX_DEV, 0)
        leaf_matrices = lax.dynamic_slice_in_dim(leaf_transfer, leaf_start, LEAF_DEV, 0)
        own_root = lax.dynamic_index_in_dim(field_root, device, 0, keepdims=False)
        field_box = jnp.einsum('krs,vs->kvr', widen(box_matrices), own_root, precision=HIGHEST) + far_box
        field_leaf = lower_field(leaf_matrices, jnp.repeat(field_box, 8, axis=0)) + far_leaf
        own_basis = lax.dynamic_slice_in_dim(basis, leaf_start, LEAF_DEV, 0)
        far_points = jnp.einsum('lar,lvr->vla', widen(own_basis), field_leaf, precision=HIGHEST)
        near_ids = lax.dynamic_slice_in_dim(near_index, leaf_start, LEAF_DEV, 0)
        gathered = point_blocks[:, near_ids]
        own_near = lax.dynamic_slice_in_dim(near_block, leaf_start, LEAF_DEV, 0)
        near_points = jnp.einsum('lnab,vlnb->vla', widen(own_near), widen(gathered), precision=HIGHEST)
        return (far_points + near_points).astype(jnp.bfloat16).reshape(NVEC, LEAF_DEV * B)

    blocks = lax.map(one_device, jnp.arange(row_count, dtype=jnp.int32))
    return blocks.transpose(1, 0, 2).reshape(NVEC, POINTS)
```

```python
import jax
import jax.numpy as jnp
from jax import lax
from jax.experimental import pallas as pl
from jax.experimental.pallas import tpu as pltpu
from jax.sharding import PartitionSpec as P

BF = jnp.bfloat16
F32 = jnp.float32
MESH = pl.DeviceIdType.MESH
NX, NZ, NC, NQ = 4, 8, 2, 4
NROWS = NX * NZ * NC
LEAF, BOX, NEAR = 64, 8, 8
FL, FB = 6, 4
TILES = LEAF + BOX + 1
CUT = 36
SLOTS = 7
GROUP = NX * NC * NQ


def rem(a, n):
    return lax.rem(a, n)


def diag(block):
    zero = jnp.zeros_like(block)
    return jnp.concatenate(
        [jnp.concatenate([block, zero], axis=1), jnp.concatenate([zero, block], axis=1)], axis=0
    )


def diag2(first, second):
    zero = jnp.zeros_like(first)
    return jnp.concatenate(
        [jnp.concatenate([first, zero], axis=1), jnp.concatenate([zero, second], axis=1)], axis=0
    )


def dot_nn(a, b):
    return lax.dot_general(a, b, (((1,), (0,)), ((), ())), preferred_element_type=F32)


def dot_nt(a, b):
    return lax.dot_general(a, b, (((1,), (1,)), ((), ())), preferred_element_type=F32)


def split_pair(wide):
    low, high = wide[:16], wide[16:]
    low_turned, high_turned = pltpu.roll(low, 64, 1), pltpu.roll(high, 64, 1)
    first = lax.broadcasted_iota(jnp.int32, (16, 128), 1) < 64
    return jnp.where(first, low, high_turned), jnp.where(first, low_turned, high)


def join_pair(even, odd):
    even_turned, odd_turned = pltpu.roll(even, 64, 1), pltpu.roll(odd, 64, 1)
    first = lax.broadcasted_iota(jnp.int32, (16, 128), 1) < 64
    return jnp.concatenate(
        [jnp.where(first, even, odd_turned), jnp.where(first, even_turned, odd)], axis=0
    )


def exchange_kernel(
    points, basis, leaf_transfer, box_transfer, table,
    recv, near,
    *scratch,
):
    held, scratch = scratch[:NZ], scratch[NZ:]
    tables, staged, own_points, index = scratch[:4]
    (
        tab_send, tab_recv, ring_send, ring_recv, out_send, out_recv, self_sem,
        near_send, near_recv, near_self, index_sem,
    ) = scratch[4:]
    mine = held[0]
    me, v = lax.axis_index("rows"), lax.axis_index("cols")
    c = rem(me, NC)
    z = rem(me // NC, NZ)
    x = me // (NC * NZ)

    def row(xx, zz, cc):
        return (xx * NZ + zz) * NC + cc

    def target(k):
        dx, dc, dq = k // (NC * NQ), rem(k // NQ, NC), rem(k, NQ)
        return row(rem(x + dx, NX), z, rem(c + dc, NC)), rem(v + dq, NQ), dq

    z_up, z_down = row(x, rem(z + 1, NZ), c), row(x, rem(z + NZ - 1, NZ), c)
    far_side = rem(me + 2 * c - 1 + NROWS, NROWS)
    barrier = pltpu.get_barrier_semaphore()

    @pl.loop(1, GROUP)
    def _(k):
        d, q, _ = target(k)
        pl.semaphore_signal(barrier, inc=1, device_id=(d, q), device_id_type=MESH)

    for d in (z_up, z_down, far_side):
        pl.semaphore_signal(barrier, inc=1, device_id=(d, v), device_id_type=MESH)
    tables[0, 0] = table[...]
    pl.semaphore_wait(barrier, GROUP + 2)

    for step in range(1, NQ):
        pltpu.make_async_remote_copy(
            src_ref=table, dst_ref=tables.at[0, NQ - step],
            send_sem=tab_send, recv_sem=tab_recv,
            device_id=(me, rem(v + step, NQ)), device_id_type=MESH,
        ).start()

    @pl.loop(0, BOX)
    def _(k):
        pairs = []
        for j in range(4):
            pair = k * 4 + j
            block = points[:, pl.ds(pl.multiple_of(pair * 128, 128), 128)]
            even, odd = split_pair(block.astype(F32))
            own_points[2 * pair] = even.astype(BF)
            own_points[2 * pair + 1] = odd.astype(BF)
            coef = dot_nn(block, diag2(basis[2 * pair], basis[2 * pair + 1]))
            pairs.append(coef.astype(BF))
            even, odd = split_pair(coef)
            mine[2 * pair] = even.astype(BF)
            mine[2 * pair + 1] = odd.astype(BF)
        wide = jnp.concatenate(pairs, axis=1)
        box = dot_nn(wide, leaf_transfer[pl.ds(k * 8, 8)].reshape(512, 64))
        mine[LEAF + k] = jnp.concatenate([box[:16], box[16:]], axis=1).astype(BF)

    first = lax.broadcasted_iota(jnp.int32, (16, 128), 1) < 64
    total = jnp.zeros((32, 64), F32)
    for k in range(BOX):
        tile = mine[LEAF + k].astype(F32)
        low = tile[:, :64]
        high = pltpu.roll(tile, 64, 1)[:, :64]
        total += dot_nn(jnp.concatenate([low, high], axis=0).astype(BF), box_transfer[k])
    mine[LEAF + BOX] = jnp.concatenate([total[:16], total[16:]], axis=1).astype(BF)

    pltpu.make_async_copy(tables.at[0, pl.ds(1, NQ - 1)], tables.at[0, pl.ds(1, NQ - 1)], tab_recv).wait()
    pltpu.make_async_copy(tables.at[0, pl.ds(1, NQ - 1)], tables.at[0, pl.ds(1, NQ - 1)], tab_send).wait()

    def ring(way, step, piece):
        if way == 0:
            src, dst, to = (NZ - step + 1) % NZ, NZ - step, z_up
        else:
            src, dst, to = step - 1, step, z_down
        if piece == 2:
            src_ref, dst_ref = tables.at[src], tables.at[dst]
        else:
            part = pl.ds(0, CUT) if piece == 0 else pl.ds(CUT, TILES - CUT)
            src_ref, dst_ref = held[src].at[part], held[dst].at[part]
        return pltpu.make_async_remote_copy(
            src_ref=src_ref, dst_ref=dst_ref,
            send_sem=ring_send.at[way, step - 1, piece], recv_sem=ring_recv.at[dst, piece],
            device_id=(to, v), device_id_type=MESH,
        )

    def parts(step):
        if step < NZ // 2:
            return [(way, piece) for piece in (2, 0, 1) for way in (0, 1)]
        return [(0, 2), (0, 0), (1, 1)]

    for way, piece in parts(1):
        ring(way, 1, piece).start()

    near_up = pltpu.make_async_remote_copy(
        src_ref=own_points, dst_ref=near.at[0], send_sem=near_send.at[0], recv_sem=near_recv.at[0],
        device_id=(rem(me + 1, NROWS), v), device_id_type=MESH,
    )
    near_down = pltpu.make_async_remote_copy(
        src_ref=own_points, dst_ref=near.at[2], send_sem=near_send.at[1], recv_sem=near_recv.at[1],
        device_id=(rem(me + NROWS - 1, NROWS), v), device_id_type=MESH,
    )
    near_here = pltpu.make_async_copy(own_points, near.at[1], near_self)

    def pack(off):
        fetch = pltpu.make_async_copy(tables.at[off], index.at[off], index_sem)
        fetch.start()
        fetch.wait()
        source = row(x, rem(z + off, NZ), c)

        def fill(k):
            d, q, dq = target(k)
            hi, lo = d // 8, rem(d, 8) * 16
            for j in range(SLOTS - 1):
                tile = jnp.maximum(index[off, dq, hi, lo + j], 0)
                if j >= 4:
                    tile = tile + LEAF
                staged[k, off, j] = held[off][tile]
            staged[k, off, SLOTS - 1] = held[off][LEAF + BOX]
            return d, q

        @pl.loop(1, GROUP)
        def _(k):
            d, q = fill(k)
            pltpu.make_async_remote_copy(
                src_ref=staged.at[k, off], dst_ref=recv.at[v, source],
                send_sem=out_send, recv_sem=out_recv, device_id=(d, q), device_id_type=MESH,
            ).start()

        fill(0)
        pltpu.make_async_copy(staged.at[0, off], recv.at[v, source], self_sem).start()

    pack(0)
    near_up.start()
    near_down.start()
    near_here.start()
    for step in range(1, NZ // 2 + 1):
        for way, piece in parts(step):
            ring(way, step, piece).wait_recv()
            if (way, piece) in parts(step + 1) and step < NZ // 2:
                ring(way, step + 1, piece).start()
        pack(NZ - step)
        if step < NZ // 2:
            pack(step)

    for step in range(1, NZ // 2 + 1):
        for way, piece in parts(step):
            ring(way, step, piece).wait_send()
    others = staged.at[pl.ds(1, GROUP - 1)]
    pltpu.make_async_copy(others, others, out_send).wait()
    pltpu.make_async_copy(others, others, out_recv).wait()
    pltpu.make_async_copy(staged.at[0], staged.at[0], self_sem).wait()
    near_here.wait()
    near_up.wait()
    near_down.wait()


def exchange(points, basis, leaf_transfer, box_transfer, table):
    return pl.pallas_call(
        exchange_kernel,
        out_shape=(
            jax.ShapeDtypeStruct((NQ, NROWS, SLOTS, 16, 128), BF),
            jax.ShapeDtypeStruct((3, LEAF, 16, 128), BF),
        ),
        in_specs=[pl.BlockSpec(memory_space=pltpu.VMEM)] * 5,
        out_specs=(pl.BlockSpec(memory_space=pl.ANY), pl.BlockSpec(memory_space=pl.ANY)),
        scratch_shapes=[
            *[pltpu.VMEM((TILES, 16, 128), BF)] * NZ,
            pltpu.VMEM((NZ, NQ, 8, 128), jnp.int32),
            pltpu.VMEM((GROUP, NZ, SLOTS, 16, 128), BF),
            pltpu.VMEM((LEAF, 16, 128), BF),
            pltpu.SMEM((NZ, NQ, 8, 128), jnp.int32),
            pltpu.SemaphoreType.DMA,
            pltpu.SemaphoreType.DMA,
            pltpu.SemaphoreType.DMA((2, NZ // 2, 3)),
            pltpu.SemaphoreType.DMA((NZ, 3)),
            pltpu.SemaphoreType.DMA,
            pltpu.SemaphoreType.DMA,
            pltpu.SemaphoreType.DMA,
            pltpu.SemaphoreType.DMA((2,)),
            pltpu.SemaphoreType.DMA((2,)),
            pltpu.SemaphoreType.DMA,
            pltpu.SemaphoreType.DMA,
        ],
        compiler_params=pltpu.CompilerParams(
            collective_id=0, has_side_effects=True, vmem_limit_bytes=48 * 2**20
        ),
        name="exchange",
    )(points, basis, leaf_transfer, box_transfer, table)


def far_kernel(
    place, leaf_far, box_far, coarse_far,
    recv, leaf_coupling, box_coupling, coarse_coupling, leaf_transfer, box_transfer, coarse_transfer,
    out, root_field, coarse_blocks, sems,
):
    step = pl.program_id(0)
    d = place[0]

    def slot(p, j):
        return recv[:, p, j].reshape(64, 128)

    @pl.when(step == 0)
    def _():
        nodes = (d // 4, NROWS // 4 + d // 2, 3 * NROWS // 4 + d)
        copies = [
            pltpu.make_async_copy(coarse_coupling.at[n], coarse_blocks.at[i], sems.at[i])
            for i, n in enumerate(nodes)
        ]
        for copy in copies:
            copy.start()
        half = NROWS // 2

        def root(n):
            return slot(n, SLOTS - 1)

        def mid(n):
            both = dot_nn(root(2 * n), diag(coarse_transfer[half + 2 * n]))
            both += dot_nn(root(2 * n + 1), diag(coarse_transfer[half + 2 * n + 1]))
            return both.astype(BF)

        def top(n):
            both = dot_nn(mid(2 * n), diag(coarse_transfer[2 * n]))
            both += dot_nn(mid(2 * n + 1), diag(coarse_transfer[2 * n + 1]))
            return both.astype(BF)

        for copy in copies:
            copy.wait()
        field = jnp.zeros((64, 128), F32)
        starts = (0, NROWS // 4, 3 * NROWS // 4)
        for level, make in enumerate((top, mid, root)):
            if level == 1:
                field = dot_nt(field.astype(BF), diag(coarse_transfer[d // 2]))
            if level == 2:
                field = dot_nt(field.astype(BF), diag(coarse_transfer[half + d]))
            for e in range(2):
                partner = coarse_far[nodes[level], e] - starts[level]
                field += dot_nt(make(partner), diag(coarse_blocks[level, e]))
        root_field[...] = field.astype(BF)

    box = dot_nt(root_field[...], diag(box_transfer[0]))
    for e in range(FB):
        entry = box_far[step, e]
        box += dot_nt(slot(entry // 2, 4 + rem(entry, 2)), diag(box_coupling[0, e]))
    box = box.astype(BF)

    for l in range(8):
        left, right = [box], [diag(leaf_transfer[l])]
        for e in range(FL):
            entry = leaf_far[step * 8 + l, e]
            left.append(slot(entry // 4, rem(entry, 4)))
            right.append(diag(leaf_coupling[l, e]))
        field = dot_nt(jnp.concatenate(left, axis=1), jnp.concatenate(right, axis=1))
        out[:, l] = field.astype(BF).reshape(NQ, 16, 128)


def far(place, leaf_far, box_far, coarse_far, recv, leaf_coupling, box_coupling, coarse_coupling,
        leaf_transfer, box_transfer, coarse_transfer):
    whole = pl.BlockSpec(memory_space=pltpu.VMEM)
    return pl.pallas_call(
        far_kernel,
        out_shape=jax.ShapeDtypeStruct((NQ, LEAF, 16, 128), BF),
        grid_spec=pltpu.PrefetchScalarGridSpec(
            num_scalar_prefetch=4,
            grid=(BOX,),
            in_specs=[
                whole,
                pl.BlockSpec((8, FL, 64, 64), lambda i, *_: (i, 0, 0, 0)),
                pl.BlockSpec((1, FB, 64, 64), lambda i, *_: (i, 0, 0, 0)),
                pl.BlockSpec(memory_space=pl.ANY),
                pl.BlockSpec((8, 64, 64), lambda i, *_: (i, 0, 0)),
                pl.BlockSpec((1, 64, 64), lambda i, *_: (i, 0, 0)),
                whole,
            ],
            out_specs=pl.BlockSpec((NQ, 8, 16, 128), lambda i, *_: (0, i, 0, 0)),
            scratch_shapes=[
                pltpu.VMEM((64, 128), BF),
                pltpu.VMEM((3, 2, 64, 64), BF),
                pltpu.SemaphoreType.DMA((3,)),
            ],
        ),
        compiler_params=pltpu.CompilerParams(vmem_limit_bytes=48 * 2**20),
        name="far",
    )(place, leaf_far, box_far, coarse_far, recv, leaf_coupling, box_coupling, coarse_coupling,
      leaf_transfer, box_transfer, coarse_transfer)


def finish_kernel(near_index, partial, near, near_block, basis, out, arrived, near_sum, send_sem, recv_sem):
    me, v = lax.axis_index("rows"), lax.axis_index("cols")
    barrier = pltpu.get_barrier_semaphore()
    for step in range(1, NQ):
        pl.semaphore_signal(
            barrier, inc=1, device_id=(me, rem(v + step, NQ)), device_id_type=MESH
        )
    pl.semaphore_wait(barrier, NQ - 1)
    copies = []
    for step in range(1, NQ):
        q = rem(v + step, NQ)
        copy = pltpu.make_async_remote_copy(
            src_ref=partial.at[q], dst_ref=arrived.at[step - 1],
            send_sem=send_sem.at[step - 1], recv_sem=recv_sem.at[step - 1],
            device_id=(me, q), device_id_type=MESH,
        )
        copy.start()
        copies.append(copy)

    @pl.loop(0, LEAF)
    def _(l):
        left = [near[near_index[l, n]] for n in range(NEAR)]
        right = [diag(near_block[l, n]) for n in range(NEAR)]
        near_sum[l] = dot_nt(jnp.concatenate(left, axis=1), jnp.concatenate(right, axis=1))

    for copy in copies:
        copy.wait()

    @pl.loop(0, LEAF // 2)
    def _(j):
        pair = []
        for t in range(2):
            l = 2 * j + t
            field = partial[v, l].astype(F32)
            for step in range(NQ - 1):
                field += arrived[step, l].astype(F32)
            pair.append(dot_nt(field.astype(BF), diag(basis[l])) + near_sum[l])
        out[:, pl.ds(pl.multiple_of(j * 128, 128), 128)] = join_pair(*pair).astype(BF)


def finish(near_index, partial, near, near_block, basis):
    vmem = pl.BlockSpec(memory_space=pltpu.VMEM)
    return pl.pallas_call(
        finish_kernel,
        out_shape=jax.ShapeDtypeStruct((32, LEAF * 64), BF),
        in_specs=[pl.BlockSpec(memory_space=pltpu.SMEM)] + [vmem] * 4,
        out_specs=vmem,
        scratch_shapes=[
            pltpu.VMEM((NQ - 1, LEAF, 16, 128), BF),
            pltpu.VMEM((LEAF, 16, 128), F32),
            pltpu.SemaphoreType.DMA((NQ - 1,)),
            pltpu.SemaphoreType.DMA((NQ - 1,)),
        ],
        compiler_params=pltpu.CompilerParams(
            collective_id=1, has_side_effects=True, vmem_limit_bytes=48 * 2**20
        ),
        name="finish",
    )(near_index, partial, near, near_block, basis)


def body(
    points, basis, leaf_transfer, box_transfer, coarse_transfer, send_leaf, leaf_far, leaf_coupling,
    send_box, box_far, box_coupling, coarse_far, coarse_coupling, near_index, near_block,
):
    me = lax.axis_index("rows")
    table = jnp.concatenate(
        [send_leaf, send_box, jnp.zeros((NROWS, 10), jnp.int32)], axis=1
    ).reshape(8, 128)
    recv, near = exchange(points, basis, leaf_transfer, box_transfer, table)
    partial = far(
        jnp.full((1,), me, jnp.int32), leaf_far, box_far, coarse_far, recv, leaf_coupling,
        box_coupling, coarse_coupling, leaf_transfer, box_transfer, coarse_transfer,
    )
    local = jnp.clip(near_index - (me - 1) * LEAF, 0, 3 * LEAF - 1)
    return finish(local, partial, near.reshape(3 * LEAF, 16, 128), near_block, basis)


def solution(mesh):
    return jax.shard_map(
        body,
        mesh=mesh,
        in_specs=(
            P("cols", "rows"),
            P("rows", None, None),
            P("rows", None, None),
            P("rows", None, None),
            P(),
            P("rows", "cols"),
            P("rows", "cols"),
            P("rows", "cols", None, None),
            P("rows", "cols"),
            P("rows", "cols"),
            P("rows", "cols", None, None),
            P(None, "cols"),
            P(None, "cols", None, None),
            P("rows", None),
            P("rows", None, None, None),
        ),
        out_specs=P("cols", "rows"),
        check_vma=False,
    )
```

```python
import jax
import jax.numpy as jnp
from jax import lax
from jax.experimental import pallas as pl
from jax.experimental.pallas import tpu as pltpu
from jax.sharding import PartitionSpec as P

BF = jnp.bfloat16
F32 = jnp.float32
I32 = jnp.int32
MESH = pl.DeviceIdType.MESH
NX, NZ, NC, NQ = 4, 8, 2, 4
NROWS = NX * NZ * NC
LEAF, BOX, NEAR = 64, 8, 8
FL, FB = 6, 4
TILES = LEAF + BOX + 1
TOP = BOX + 1
SLOTS = 4
GROUP = NX * NC * NQ
CHUNK = 16


def rem(a, n):
    return lax.rem(a, n)


def side(a, b):
    return jnp.concatenate([a, b], axis=1)


def diag(first, second):
    zero = jnp.zeros_like(first)
    return jnp.concatenate([side(first, zero), side(zero, second)], axis=0)


def dot_nn(a, b):
    return lax.dot_general(a, b, (((1,), (0,)), ((), ())), preferred_element_type=F32)


def dot_nt(a, b):
    return lax.dot_general(a, b, (((1,), (1,)), ((), ())), preferred_element_type=F32)


def split_pair(wide):
    low, high = wide[:16], wide[16:]
    low_turned, high_turned = pltpu.roll(low, 64, 1), pltpu.roll(high, 64, 1)
    first = lax.broadcasted_iota(I32, (16, 128), 1) < 64
    return jnp.where(first, low, high_turned), jnp.where(first, low_turned, high)


def join_pair(even, odd):
    even_turned, odd_turned = pltpu.roll(even, 64, 1), pltpu.roll(odd, 64, 1)
    first = lax.broadcasted_iota(I32, (16, 128), 1) < 64
    return jnp.concatenate(
        [jnp.where(first, even, odd_turned), jnp.where(first, even_turned, odd)], axis=0
    )


def join_tiles(even, odd):
    return join_pair(even.astype(F32), odd.astype(F32)).astype(BF)


def kernel(
    points, ints, basis_h, leaf_h, box_h, leaf_coupling, box_coupling, coarse_h, coarse_coupling,
    near_block, out, *scratch,
):
    held, scratch = scratch[:NZ], scratch[NZ:]
    (
        tables, index, lists, lists_s, ints_s, staged, recv, every, rows_out, rows_in, rows_s,
        near, near_pair, base_pair, basis_pair, weights,
        basis, leaf_transfer, box_transfer, box_raw, coarse_raw, coupling_raw, near_raw, leaf_raw,
        coarse, picked, shared, upper, part, arrived,
    ) = scratch[:30]
    (
        load, chunk_load, tab_send, tab_recv, ring_send, ring_recv, out_send, out_recv, self_sem,
        near_send, near_recv, index_sem, every_send, every_recv, every_self, sibling_recv,
        rows_send, rows_recv, shared_send, shared_recv, part_send, part_recv,
    ) = scratch[30:]
    mine = held[0]
    me, v = lax.axis_index("rows"), lax.axis_index("cols")
    c = rem(me, NC)
    z = rem(me // NC, NZ)
    x = me // (NC * NZ)

    def row(xx, zz, cc):
        return (xx * NZ + zz) * NC + cc

    def target(k):
        dx, dc, dq = k // (NC * NQ), rem(k // NQ, NC), rem(k, NQ)
        return row(rem(x + dx, NX), z, rem(c + dc, NC)), rem(v + dq, NQ), dq

    def remote(src, dst, send, arrive, d, q):
        return pltpu.make_async_remote_copy(
            src_ref=src, dst_ref=dst, send_sem=send, recv_sem=arrive,
            device_id=(d, q), device_id_type=MESH,
        )

    def settle(ref, sem):
        pltpu.make_async_copy(ref, ref, sem).wait()

    loads = [
        pltpu.make_async_copy(src, dst, load.at[i])
        for i, (src, dst) in enumerate((
            (basis_h, basis), (leaf_h, leaf_transfer), (box_h, box_transfer),
            (ints.at[pl.ds(16, 8)], ints_s), (box_coupling, box_raw),
            (coarse_coupling, coupling_raw), (coarse_h, coarse_raw),
        ))
    ]
    for copy in loads:
        copy.start()

    def chunk_copies(i):
        part_of = pl.ds(i * CHUNK, CHUNK)
        return (
            pltpu.make_async_copy(near_block.at[part_of], near_raw.at[i % 2], chunk_load.at[0, i % 2]),
            pltpu.make_async_copy(leaf_coupling.at[part_of], leaf_raw.at[i % 2], chunk_load.at[1, i % 2]),
        )

    z_up, z_down = row(x, rem(z + 1, NZ), c), row(x, rem(z + NZ - 1, NZ), c)
    sibling = row(x, z, 1 - c)
    far_side = rem(me + 2 * c - 1 + NROWS, NROWS)
    barrier = pltpu.get_barrier_semaphore()

    @pl.loop(1, GROUP)
    def _(k):
        d, q, _ = target(k)
        pl.semaphore_signal(barrier, inc=1, device_id=(d, q), device_id_type=MESH)

    for d in (z_up, z_down, far_side):
        pl.semaphore_signal(barrier, inc=1, device_id=(d, v), device_id_type=MESH)
    tables[0, 0] = ints[pl.ds(0, 8)]
    lists[0] = ints[pl.ds(8, 8)]

    @pl.loop(0, LEAF // 2)
    def _(j):
        block = points[:, pl.ds(pl.multiple_of(j * 128, 128), 128)]
        even, odd = split_pair(block.astype(F32))
        near[LEAF + 2 * j] = even.astype(BF)
        near[LEAF + 2 * j + 1] = odd.astype(BF)

    pl.semaphore_wait(barrier, GROUP + 2)

    for step in range(1, NQ):
        q = rem(v + step, NQ)
        remote(ints.at[pl.ds(0, 8)], tables.at[0, NQ - step], tab_send.at[0], tab_recv.at[0], me, q).start()
        remote(ints.at[pl.ds(8, 8)], lists.at[NQ - step], tab_send.at[1], tab_recv.at[1], me, q).start()
    own_near = near.at[pl.ds(LEAF, LEAF)]
    near_copies = (
        remote(own_near, near.at[pl.ds(0, LEAF)], near_send.at[0], near_recv.at[0], rem(me + 1, NROWS), v),
        remote(own_near, near.at[pl.ds(2 * LEAF, LEAF)], near_send.at[1], near_recv.at[1], rem(me + NROWS - 1, NROWS), v),
    )

    loads[0].wait()
    loads[1].wait()
    loads[2].wait()

    def coefficients(k):
        for j in range(4):
            pair = k * 4 + j
            block = points[:, pl.ds(pl.multiple_of(pair * 128, 128), 128)]
            wide = diag(basis[2 * pair], basis[2 * pair + 1])
            basis_pair[pair] = wide
            coef = dot_nn(block, wide)
            near_pair[pair] = coef
            even, odd = split_pair(coef)
            mine[2 * pair] = even.astype(BF)
            mine[2 * pair + 1] = odd.astype(BF)

    pl.loop(0, BOX)(coefficients)

    settle(tables.at[0, pl.ds(1, NQ - 1)], tab_recv.at[0])

    PIECES = {0: pl.ds(0, 32), 1: pl.ds(32, 32), 3: pl.ds(LEAF, TOP)}

    def ring(way, step, piece):
        if way == 0:
            src, dst, to = (NZ - step + 1) % NZ, NZ - step, z_up
        else:
            src, dst, to = step - 1, step, z_down
        if piece == 2:
            src_ref, dst_ref = tables.at[src], tables.at[dst]
        else:
            src_ref, dst_ref = held[src].at[PIECES[piece]], held[dst].at[PIECES[piece]]
        return remote(
            src_ref, dst_ref, ring_send.at[way, step - 1, piece], ring_recv.at[dst, piece], to, v
        )

    def parts(step):
        if step < NZ // 2:
            return [(way, piece) for piece in (2, 0, 1, 3) for way in (0, 1)]
        return [(0, 2), (0, 0), (1, 1), (1, 3)]

    for way, piece in parts(1):
        if piece != 3:
            ring(way, 1, piece).start()
    for copy in near_copies:
        copy.start()
    for i in range(2):
        for copy in chunk_copies(i):
            copy.start()

    def box_coefficients(k):
        wide = jnp.concatenate([near_pair[4 * k + j].astype(BF) for j in range(4)], axis=1)
        box = dot_nn(wide, leaf_transfer[pl.ds(k * 8, 8)].reshape(512, 64))
        mine[LEAF + k] = side(box[:16], box[16:]).astype(BF)

    def pack_slots(off):
        fetch = pltpu.make_async_copy(tables.at[off], index.at[off], index_sem)
        fetch.start()
        fetch.wait()
        source = row(x, rem(z + off, NZ), c)

        def fill(k):
            d, q, dq = target(k)
            hi, lo = d // 8, rem(d, 8) * 16
            for j in range(SLOTS):
                tile = jnp.maximum(index[off, dq, hi, lo + j], 0)
                staged[k, off, j] = held[off][tile]
            return d, q

        @pl.loop(1, GROUP)
        def _(k):
            d, q = fill(k)
            remote(staged.at[k, off], recv.at[v, source], out_send, out_recv, d, q).start()

        fill(0)
        pltpu.make_async_copy(staged.at[0, off], recv.at[v, source], self_sem).start()

    def block_of(cc, xx):
        return (cc * NX + xx) * NZ

    def pack_boxes(off):
        place = block_of(c, x) + rem(z + off, NZ)
        source = held[off].at[pl.ds(LEAF, TOP)]
        for dx in range(1, NX):
            remote(
                source, every.at[place], every_send, every_recv.at[dx - 1],
                row(rem(x + dx, NX), z, c), v,
            ).start()
        remote(source, every.at[place], every_send, sibling_recv.at[0], sibling, v).start()
        pltpu.make_async_copy(source, every.at[place], every_self).start()
        for dx in range(NX):
            line = rem(x + dx, NX) * 2 + z // 4
            for q in range(NQ):
                rows_out[dx, rem(z + off, NZ), pl.ds(q, 1), :] = tables[off, q, pl.ds(line, 1), :]

    pack_slots(0)

    pl.loop(0, BOX)(box_coefficients)
    total = jnp.zeros((32, 64), F32)
    for k in range(0, BOX, 2):
        pair = join_tiles(mine[LEAF + k], mine[LEAF + k + 1])
        total += dot_nn(pair, box_transfer[pl.ds(k, 2)].reshape(128, 64))
    mine[LEAF + BOX] = side(total[:16], total[16:]).astype(BF)
    for way, piece in parts(1):
        if piece == 3:
            ring(way, 1, piece).start()
    pack_boxes(0)

    loads[4].wait()

    @pl.loop(0, BOX)
    def _(k):
        for m in range(2):
            shared[0, 2 * k + m] = side(box_raw[k, 2 * m], box_raw[k, 2 * m + 1])

    for step in range(1, NQ):
        remote(
            shared.at[0, pl.ds(0, 16)], shared.at[NQ - step, pl.ds(0, 16)],
            shared_send.at[0], shared_recv.at[0], me, rem(v + step, NQ),
        ).start()
    loads[3].wait()

    def chunk(i):
        for copy in chunk_copies(i):
            copy.wait()
        slot = i % 2

        @pl.loop(0, CHUNK // 2)
        def _(j):
            sides = []
            for t in range(2):
                l = 2 * j + t
                first = (i * CHUNK + l) * NEAR
                hi, lo = 3 + first // 128, rem(first, 128)
                left, right = [], []
                for n in range(0, NEAR, 2):
                    left.append(join_tiles(near[ints_s[hi, lo + n]], near[ints_s[hi, lo + n + 1]]))
                    right.append(side(near_raw[slot, l, n], near_raw[slot, l, n + 1]))
                sides.append(dot_nt(jnp.concatenate(left, axis=1), jnp.concatenate(right, axis=1)))
                for e in range(FL):
                    block = leaf_raw[slot, l, e]
                    weights[i * CHUNK + l, :, pl.ds(e * 128, 128)] = diag(block, block)
            near_pair[i * (CHUNK // 2) + j] = side(*sides)

        if i + 2 < LEAF // CHUNK:
            for copy in chunk_copies(i + 2):
                copy.start()

    for step in range(1, NZ // 2 + 1):
        for way, piece in parts(step):
            ring(way, step, piece).wait_recv()
            if step < NZ // 2 and (way, piece) in parts(step + 1):
                ring(way, step + 1, piece).start()
        offs = (NZ - step, step) if step < NZ // 2 else (step,)
        for off in offs:
            pack_boxes(off)
            pack_slots(off)
        if step == 1:
            for copy in near_copies:
                copy.wait_recv()
        if step < NZ // 2:
            chunk(step - 1)

    for k in range(1, NX * NC):
        dx, dc = k // NC, k % NC
        remote(
            rows_out.at[dx], rows_in.at[c * NX + x], rows_send, rows_recv,
            row(rem(x + dx, NX), z, rem(c + dc, NC)), v,
        ).start()
    rows_in[c * NX + x] = rows_out[0]
    chunk(3)

    loads[5].wait()
    levels = (me // 4, NROWS // 4 + me // 2, 3 * NROWS // 4 + me)
    line = lax.broadcasted_iota(I32, (8, 112), 0)
    node = lax.broadcasted_iota(I32, (8, 112), 1)
    chosen = jnp.zeros((8, 112), F32)
    for i, n in enumerate(levels):
        chosen = jnp.where((line == i) & (node == n), 1.0, chosen)
    chosen = chosen.astype(BF)

    @pl.loop(0, 64)
    def _(r):
        for e in range(2):
            picked[e, r] = dot_nt(chosen, coupling_raw[e, r])

    for i in range(3):
        shared[0, 16 + i] = side(picked[0, :, i, :], picked[1, :, i, :]).astype(BF)
    for step in range(1, NQ):
        remote(
            shared.at[0, pl.ds(16, 3)], shared.at[NQ - step, pl.ds(16, 3)],
            shared_send.at[1], shared_recv.at[1], me, rem(v + step, NQ),
        ).start()

    loads[6].wait()
    same = lax.broadcasted_iota(I32, (96, 96), 0) == lax.broadcasted_iota(I32, (96, 96), 1)
    eye = jnp.where(same, 1.0, 0.0).astype(BF)

    @pl.loop(0, 64)
    def _(r):
        coarse[r] = dot_nt(eye, coarse_raw[r])

    for dx in range(1, NX):
        here = every.at[pl.ds(block_of(c, rem(x + NX - dx, NX)), NZ)]
        settle(here, every_recv.at[dx - 1])
        remote(here, here, every_send, sibling_recv.at[dx], sibling, v).start()

    settle(staged.at[pl.ds(1, GROUP - 1)], out_recv)
    settle(staged.at[0], self_sem)

    @pl.loop(0, BOX)
    def _(k):
        for i in range(8):
            l = k * 8 + i
            left = []
            for e in range(FL):
                f = l * FL + e
                entry = ints_s[f // 128, rem(f, 128)]
                left.append(recv[:, entry // SLOTS, rem(entry, SLOTS)].reshape(64, 128))
            field = dot_nt(jnp.concatenate(left, axis=1), weights[l])
            part[:, l] = field.astype(BF).reshape(NQ, 16, 128)
        for step in range(1, NQ):
            q = rem(v + step, NQ)
            span = pl.ds(pl.multiple_of(k * 8, 8), 8)
            remote(
                part.at[q, span], arrived.at[step - 1, span], part_send, part_recv.at[k], me, q
            ).start()

    settle(lists.at[pl.ds(1, NQ - 1)], tab_recv.at[1])
    settle(shared.at[pl.ds(1, NQ - 1), pl.ds(0, 16)], shared_recv.at[0])
    settle(shared.at[pl.ds(1, NQ - 1), pl.ds(16, 3)], shared_recv.at[1])
    settle(rows_in.at[pl.ds(0, NX * NC - 1)], rows_recv)
    fetches = [
        pltpu.make_async_copy(lists, lists_s, load.at[0]),
        pltpu.make_async_copy(rows_in, rows_s, load.at[1]),
    ]
    for fetch in fetches:
        fetch.start()
    settle(every.at[pl.ds(0, NZ)], every_self)
    for dx in range(NX):
        settle(every.at[pl.ds(0, NZ)], sibling_recv.at[dx])
    for fetch in fetches:
        fetch.wait()

    def matrix(n):
        return coarse[:, n, :].astype(BF)

    def place_of(p):
        return block_of(rem(p, NC), p // (NC * NZ)) + rem(p // NC, NZ)

    @pl.loop(0, NROWS // 2)
    def _(n):
        pair = join_tiles(every[place_of(2 * n), BOX], every[place_of(2 * n + 1), BOX])
        pile = jnp.concatenate([matrix(32 + 2 * n), matrix(33 + 2 * n)], axis=0)
        upper[16 + n] = dot_nn(pair, pile).astype(BF)

    @pl.loop(0, NROWS // 4)
    def _(n):
        pair = side(upper[16 + 2 * n], upper[17 + 2 * n])
        pile = jnp.concatenate([matrix(2 * n), matrix(2 * n + 1)], axis=0)
        upper[n] = dot_nn(pair, pile).astype(BF)

    field = jnp.zeros((32, 64), F32)
    for level in range(3):
        if level == 1:
            field = dot_nt(field.astype(BF), matrix(me // 2))
        if level == 2:
            field = dot_nt(field.astype(BF), matrix(32 + me))
        for q in range(NQ):
            f = 32 + levels[level] * 2
            a, b = (lists_s[q, (f + e) // 128, rem(f + e, 128)] for e in range(2))
            if level < 2:
                pair = side(upper[a], upper[b])
            else:
                pair = join_tiles(every[place_of(jnp.maximum(a - 48, 0)), BOX], every[place_of(jnp.maximum(b - 48, 0)), BOX])
            field += dot_nt(pair, shared[q, 16 + level])
    root = field.astype(BF)
    column = (rem(z, 4) * 2 + c) * 16 + SLOTS

    @pl.loop(0, BOX)
    def _(k):
        left, right = [], []
        for q in range(NQ):
            for m in range(FB // 2):
                tiles = []
                for e in range(2):
                    entry = lists_s[q, 0, k * FB + 2 * m + e]
                    p = entry // 2
                    source = rem(p, NC) * NX + p // (NC * NZ)
                    zz = rem(p // NC, NZ)
                    number = rows_s[source, zz, q, column + rem(entry, 2)]
                    tiles.append(every[source * NZ + zz, jnp.maximum(number, 0)])
                left.append(join_tiles(*tiles))
                right.append(shared[q, 2 * k + m])
        box = dot_nt(root, box_transfer[k])
        box += dot_nt(jnp.concatenate(left, axis=1), jnp.concatenate(right, axis=1))
        wide = dot_nt(box.astype(BF), leaf_transfer[pl.ds(k * 8, 8)].reshape(512, 64))
        for j in range(4):
            base_pair[4 * k + j] = wide[:, j * 128 : (j + 1) * 128]

    @pl.loop(0, BOX)
    def _(k):
        span = pl.ds(pl.multiple_of(k * 8, 8), 8)
        settle(arrived.at[:, span], part_recv.at[k])
        for i in range(4):
            j = 4 * k + i
            fields = []
            for t in range(2):
                field = part[v, 2 * j + t].astype(F32)
                for step in range(NQ - 1):
                    field += arrived[step, 2 * j + t].astype(F32)
                fields.append(field)
            pair = (join_pair(*fields) + base_pair[j]).astype(BF)
            value = dot_nt(pair, basis_pair[j]) + near_pair[j]
            out[:, pl.ds(pl.multiple_of(j * 128, 128), 128)] = value.astype(BF)

    for step in range(1, NZ // 2 + 1):
        for way, piece in parts(step):
            ring(way, step, piece).wait_send()
    settle(tables.at[0, pl.ds(1, NQ - 1)], tab_send.at[0])
    settle(lists.at[pl.ds(1, NQ - 1)], tab_send.at[1])
    settle(staged.at[pl.ds(1, GROUP - 1)], out_send)
    settle(every.at[pl.ds(0, NZ * NX + NZ * (NX - 1))], every_send)
    settle(rows_in.at[pl.ds(0, NX * NC - 1)], rows_send)
    settle(shared.at[pl.ds(1, NQ - 1), pl.ds(0, 16)], shared_send.at[0])
    settle(shared.at[pl.ds(1, NQ - 1), pl.ds(16, 3)], shared_send.at[1])
    settle(arrived, part_send)
    for copy in near_copies:
        copy.wait_send()


def product(points, ints, *arrays):
    vmem, hbm = pl.BlockSpec(memory_space=pltpu.VMEM), pl.BlockSpec(memory_space=pl.ANY)
    dma = pltpu.SemaphoreType.DMA
    return pl.pallas_call(
        kernel,
        out_shape=jax.ShapeDtypeStruct((32, LEAF * 64), BF),
        in_specs=[vmem, vmem] + [hbm] * 8,
        out_specs=vmem,
        scratch_shapes=[
            *[pltpu.VMEM((TILES, 16, 128), BF)] * NZ,
            pltpu.VMEM((NZ, NQ, 8, 128), I32),
            pltpu.SMEM((NZ, NQ, 8, 128), I32),
            pltpu.VMEM((NQ, 8, 128), I32),
            pltpu.SMEM((NQ, 8, 128), I32),
            pltpu.SMEM((8, 128), I32),
            pltpu.VMEM((GROUP, NZ, SLOTS, 16, 128), BF),
            pltpu.VMEM((NQ, NROWS, SLOTS, 16, 128), BF),
            pltpu.VMEM((NROWS, TOP, 16, 128), BF),
            pltpu.VMEM((NX, NZ, NQ, 128), I32),
            pltpu.VMEM((NX * NC, NZ, NQ, 128), I32),
            pltpu.SMEM((NX * NC, NZ, NQ, 128), I32),
            pltpu.VMEM((3 * LEAF, 16, 128), BF),
            pltpu.VMEM((LEAF // 2, 32, 128), F32),
            pltpu.VMEM((LEAF // 2, 32, 128), F32),
            pltpu.VMEM((LEAF // 2, 128, 128), BF),
            pltpu.VMEM((LEAF, 128, FL * 128), BF),
            pltpu.VMEM((LEAF, 64, 64), BF),
            pltpu.VMEM((LEAF, 64, 64), BF),
            pltpu.VMEM((BOX, 64, 64), BF),
            pltpu.VMEM((BOX, FB, 64, 64), BF),
            pltpu.VMEM((64, 64, 96), BF),
            pltpu.VMEM((2, 64, 64, 112), BF),
            pltpu.VMEM((2, CHUNK, NEAR, 64, 64), BF),
            pltpu.VMEM((2, CHUNK, FL, 64, 64), BF),
            pltpu.VMEM((64, 96, 64), F32),
            pltpu.VMEM((2, 64, 8, 64), F32),
            pltpu.VMEM((NQ, 19, 64, 128), BF),
            pltpu.VMEM((48, 32, 64), BF),
            pltpu.VMEM((NQ, LEAF, 16, 128), BF),
            pltpu.VMEM((NQ - 1, LEAF, 16, 128), BF),
            dma((7,)),
            dma((2, 2)),
            dma((2,)),
            dma((2,)),
            dma((2, NZ // 2, 4)),
            dma((NZ, 4)),
            dma,
            dma,
            dma,
            dma((2,)),
            dma((2,)),
            dma,
            dma,
            dma((NX - 1,)),
            dma,
            dma((NX,)),
            dma,
            dma,
            dma((2,)),
            dma((2,)),
            dma,
            dma((BOX,)),
        ],
        compiler_params=pltpu.CompilerParams(
            collective_id=0, has_side_effects=True, vmem_limit_bytes=60 * 2**20
        ),
        name="product",
    )(points, ints, *arrays)


def body(
    points, basis, leaf_transfer, box_transfer, coarse_transfer, send_leaf, leaf_far, leaf_coupling,
    send_box, box_far, box_coupling, coarse_far, coarse_coupling, near_index, near_block,
):
    me = lax.axis_index("rows")
    local = jnp.clip(near_index - (me - 1) * LEAF, 0, 3 * LEAF - 1)
    table = jnp.concatenate([send_leaf, send_box, jnp.zeros((NROWS, 10), I32)], axis=1)
    ints = jnp.concatenate([
        table.reshape(-1), box_far.reshape(-1), coarse_far.reshape(-1), jnp.zeros((768,), I32),
        leaf_far.reshape(-1), local.reshape(-1), jnp.zeros((128,), I32),
    ]).reshape(24, 128)
    return product(
        points, ints, basis, leaf_transfer, box_transfer, leaf_coupling, box_coupling,
        coarse_transfer.transpose(1, 2, 0), coarse_coupling.transpose(1, 2, 3, 0), near_block,
    )


def solution(mesh):
    return jax.shard_map(
        body,
        mesh=mesh,
        in_specs=(
            P("cols", "rows"),
            P("rows", None, None),
            P("rows", None, None),
            P("rows", None, None),
            P(),
            P("rows", "cols"),
            P("rows", "cols"),
            P("rows", "cols", None, None),
            P("rows", "cols"),
            P("rows", "cols"),
            P("rows", "cols", None, None),
            P(None, "cols"),
            P(None, "cols", None, None),
            P("rows", None),
            P("rows", None, None, None),
        ),
        out_specs=P("cols", "rows"),
        check_vma=False,
    )
```

```python
import jax
import jax.numpy as jnp
from jax import lax
from jax.experimental import pallas as pl
from jax.experimental.pallas import tpu as pltpu
from jax.sharding import PartitionSpec as P

BF = jnp.bfloat16
F32 = jnp.float32
I32 = jnp.int32
MESH = pl.DeviceIdType.MESH
NX, NZ, NC, NQ = 4, 8, 2, 4
NROWS = NX * NZ * NC
LEAF, BOX, NEAR = 64, 8, 8
FL, FB = 6, 4
TOP = BOX + 1
SLOTS = 4
GROUP = NX * NC * NQ
CHUNK = 16


def rem(a, n):
    return lax.rem(a, n)


def side(a, b):
    return jnp.concatenate([a, b], axis=1)


def diag(first, second):
    zero = jnp.zeros_like(first)
    return jnp.concatenate([side(first, zero), side(zero, second)], axis=0)


def dot_nn(a, b):
    return lax.dot_general(a, b, (((1,), (0,)), ((), ())), preferred_element_type=F32)


def dot_nt(a, b):
    return lax.dot_general(a, b, (((1,), (1,)), ((), ())), preferred_element_type=F32)


def split_pair(wide):
    low, high = wide[:16], wide[16:]
    low_turned, high_turned = pltpu.roll(low, 64, 1), pltpu.roll(high, 64, 1)
    first = lax.broadcasted_iota(I32, (16, 128), 1) < 64
    return jnp.where(first, low, high_turned), jnp.where(first, low_turned, high)


def join_pair(even, odd):
    even_turned, odd_turned = pltpu.roll(even, 64, 1), pltpu.roll(odd, 64, 1)
    first = lax.broadcasted_iota(I32, (16, 128), 1) < 64
    return jnp.concatenate(
        [jnp.where(first, even, odd_turned), jnp.where(first, even_turned, odd)], axis=0
    )


def join_tiles(even, odd):
    return join_pair(even.astype(F32), odd.astype(F32)).astype(BF)


def kernel(
    points, send_leaf, send_box, box_far, coarse_far, leaf_far, near_index, basis_h, leaf_h, box_h, leaf_coupling, box_coupling, coarse_h, coarse_coupling,
    near_block, out, *scratch,
):
    held, scratch = scratch[:NZ], scratch[NZ:]
    (
        raw, turned_raw, table, tables, compact, index, lists, lists_v, lists_s, leaf_s, near_s, staged, recv, every,
        rows_in, rows_v, rows_s,
        near, near_pair, base_pair, basis_pair, weights,
        basis, leaf_transfer, box_transfer, box_raw, coarse_raw, coupling_raw, near_raw, leaf_raw,
        coarse, picked, shared, upper, part, arrived,
    ) = scratch[:36]
    (
        load, chunk_load, tab_send, tab_recv, ring_send, ring_recv, out_send, out_recv, self_sem,
        near_send, near_recv, index_sem, every_send, every_recv, sibling_recv, box_send, box_recv,
        rows_send, rows_recv, shared_send, shared_recv, part_send, part_recv,
    ) = scratch[36:]
    mine = held[0]
    me, v = lax.axis_index("rows"), lax.axis_index("cols")
    c = rem(me, NC)
    z = rem(me // NC, NZ)
    x = me // (NC * NZ)

    def row(xx, zz, cc):
        return (xx * NZ + zz) * NC + cc

    def target(k):
        dx, dc, dq = k // (NC * NQ), rem(k // NQ, NC), rem(k, NQ)
        return row(rem(x + dx, NX), z, rem(c + dc, NC)), rem(v + dq, NQ), dq

    def remote(src, dst, send, arrive, d, q):
        return pltpu.make_async_remote_copy(
            src_ref=src, dst_ref=dst, send_sem=send, recv_sem=arrive,
            device_id=(d, q), device_id_type=MESH,
        )

    def settle(ref, sem):
        pltpu.make_async_copy(ref, ref, sem).wait()

    loads = [
        pltpu.make_async_copy(src, dst, load.at[i])
        for i, (src, dst) in enumerate((
            (basis_h, basis), (leaf_h, leaf_transfer), (box_h, box_transfer),
            (near_index, near_s), (box_coupling, box_raw),
            (coarse_coupling, coupling_raw), (coarse_h, coarse_raw), (leaf_far, leaf_s),
        ))
    ]
    for copy in loads:
        copy.start()

    def chunk_copies(i):
        part_of = pl.ds(i * CHUNK, CHUNK)
        return (
            pltpu.make_async_copy(near_block.at[part_of], near_raw.at[i % 2], chunk_load.at[0, i % 2]),
            pltpu.make_async_copy(leaf_coupling.at[part_of], leaf_raw.at[i % 2], chunk_load.at[1, i % 2]),
        )

    for i in range(2):
        for copy in chunk_copies(i):
            copy.start()

    z_up, z_down = row(x, rem(z + 1, NZ), c), row(x, rem(z + NZ - 1, NZ), c)
    sibling = row(x, z, 1 - c)
    far_side = rem(me + 2 * c - 1 + NROWS, NROWS)
    barrier = pltpu.get_barrier_semaphore()

    @pl.loop(1, GROUP)
    def _(k):
        d, q, _ = target(k)
        pl.semaphore_signal(barrier, inc=1, device_id=(d, q), device_id_type=MESH)

    for d in (z_up, z_down, far_side):
        pl.semaphore_signal(barrier, inc=1, device_id=(d, v), device_id_type=MESH)
    raw[...] = jnp.zeros((128, 128), I32)
    raw[pl.ds(0, SLOTS), pl.ds(0, NROWS)] = send_leaf[...]
    raw[pl.ds(SLOTS, 2), pl.ds(0, NROWS)] = send_box[...]
    turned_raw[...] = jnp.transpose(raw[...])
    lane = lax.broadcasted_iota(I32, (8, 128), 1)
    rows = jnp.zeros((8, 128), I32)
    for i in range(NX):
        for j in range(NC):
            column = i * 32 + j * 16
            lines = turned_raw[pl.ds(i * NZ * NC + j, NZ, stride=NC), :]
            rows = jnp.where((lane >= column) & (lane < column + 16), pltpu.roll(lines, column, 1), rows)
    table[...] = rows
    tables[0, 0] = rows
    lists[0] = jnp.zeros((8, 128), I32)
    lists[0, pl.ds(0, FB), pl.ds(0, BOX)] = box_far[...]
    lists[0, pl.ds(FB, 2), pl.ds(0, 112)] = coarse_far[...]

    @pl.loop(0, LEAF // 2)
    def _(j):
        block = points[:, pl.ds(pl.multiple_of(j * 128, 128), 128)]
        even, odd = split_pair(block.astype(F32))
        near[LEAF + 2 * j] = even.astype(BF)
        near[LEAF + 2 * j + 1] = odd.astype(BF)

    loads[0].wait()

    def coefficients(k):
        for j in range(4):
            pair = k * 4 + j
            block = points[:, pl.ds(pl.multiple_of(pair * 128, 128), 128)]
            wide = diag(basis[2 * pair], basis[2 * pair + 1])
            basis_pair[pair] = wide
            coef = dot_nn(block, wide)
            near_pair[pair] = coef
            even, odd = split_pair(coef)
            mine[2 * pair] = even.astype(BF)
            mine[2 * pair + 1] = odd.astype(BF)

    pl.loop(0, BOX)(coefficients)

    pl.semaphore_wait(barrier, GROUP + 2)

    for step in range(1, NQ):
        q = rem(v + step, NQ)
        remote(table, tables.at[0, NQ - step], tab_send.at[0], tab_recv.at[0], me, q).start()
        remote(lists.at[0], lists.at[NQ - step], tab_send.at[1], tab_recv.at[1], me, q).start()
    own_near = near.at[pl.ds(LEAF, LEAF)]
    near_copies = (
        remote(own_near, near.at[pl.ds(0, LEAF)], near_send.at[0], near_recv.at[0], rem(me + 1, NROWS), v),
        remote(own_near, near.at[pl.ds(2 * LEAF, LEAF)], near_send.at[1], near_recv.at[1], rem(me + NROWS - 1, NROWS), v),
    )

    PIECES = {0: pl.ds(0, 32), 1: pl.ds(32, 32)}

    def ring(way, step, piece):
        if way == 0:
            src, dst, to = (NZ - step + 1) % NZ, NZ - step, z_up
        else:
            src, dst, to = step - 1, step, z_down
        if piece == 2:
            src_ref, dst_ref = tables.at[src], tables.at[dst]
        else:
            src_ref, dst_ref = held[src].at[PIECES[piece]], held[dst].at[PIECES[piece]]
        return remote(
            src_ref, dst_ref, ring_send.at[way, step - 1, piece], ring_recv.at[dst, piece], to, v
        )

    def parts(step):
        if step < NZ // 2:
            return [(way, piece) for piece in (2, 0, 1) for way in (0, 1)]
        return [(0, 2), (0, 0), (1, 1)]

    for way, piece in parts(1):
        if piece != 2:
            ring(way, 1, piece).start()
    for copy in near_copies:
        copy.start()

    def box_coefficients(k):
        wide = jnp.concatenate([near_pair[4 * k + j].astype(BF) for j in range(4)], axis=1)
        box = dot_nn(wide, leaf_transfer[pl.ds(k * 8, 8)].reshape(512, 64))
        every[place, k] = side(box[:16], box[16:]).astype(BF)

    def pack_slots(off):
        for q in range(NQ):
            compact[rem(z + off, NZ), pl.ds(q, 1), :] = tables[off, q, pl.ds(z, 1), :]
        fetch = pltpu.make_async_copy(compact.at[rem(z + off, NZ)], index.at[off], index_sem)
        fetch.start()
        fetch.wait()
        source = row(x, rem(z + off, NZ), c)

        def fill(k):
            d, q, dq = target(k)
            lo = rem(x + k // (NC * NQ), NX) * 32 + rem(c + rem(k // NQ, NC), NC) * 16
            for j in range(SLOTS):
                tile = jnp.maximum(index[off, dq, lo + j], 0)
                staged[k, off, j] = held[off][tile]
            return d, q

        @pl.loop(1, GROUP)
        def _(k):
            d, q = fill(k)
            remote(staged.at[k, off], recv.at[v, source], out_send, out_recv, d, q).start()

        fill(0)
        pltpu.make_async_copy(staged.at[0, off], recv.at[v, source], self_sem).start()

    def block_of(cc, zz):
        return (cc * NZ + zz) * NX

    place = block_of(c, z) + x

    def box_ring(way, step):
        src = (NZ - step + 1) % NZ if way == 0 else step - 1
        dst = NZ - step if way == 0 else step
        block = every.at[pl.ds(block_of(c, rem(z + src, NZ)), NX)]
        return remote(
            block, block, box_send.at[way, step - 1], box_recv.at[dst], (z_up, z_down)[way], v
        )

    def box_ways(step):
        return (0, 1) if step < NZ // 2 else (0,)

    def box_step(step):
        if step == 0:
            settle(every.at[pl.ds(0, NX - 1)], every_recv)
        else:
            for way in box_ways(step):
                box_ring(way, step).wait_recv()
        if step < NZ // 2:
            for way in box_ways(step + 1):
                box_ring(way, step + 1).start()
        for off in {0: (0,), NZ // 2: (NZ // 2,)}.get(step, (NZ - step, step)):
            block = every.at[pl.ds(block_of(c, rem(z + off, NZ)), NX)]
            remote(block, block, every_send, sibling_recv, sibling, v).start()

    loads[4].wait()

    @pl.loop(0, BOX)
    def _(k):
        for m in range(2):
            shared[0, 2 * k + m] = side(box_raw[k, 2 * m], box_raw[k, 2 * m + 1])

    for step in range(1, NQ):
        remote(
            shared.at[0, pl.ds(0, 16)], shared.at[NQ - step, pl.ds(0, 16)],
            shared_send.at[0], shared_recv.at[0], me, rem(v + step, NQ),
        ).start()
    loads[1].wait()
    loads[2].wait()
    pl.loop(0, BOX)(box_coefficients)
    total = jnp.zeros((32, 64), F32)
    for k in range(0, BOX, 2):
        pair = join_tiles(every[place, k], every[place, k + 1])
        total += dot_nn(pair, box_transfer[pl.ds(k, 2)].reshape(128, 64))
    every[place, BOX] = side(total[:16], total[16:]).astype(BF)
    for dx in range(1, NX):
        remote(
            every.at[place], every.at[place], every_send, every_recv, row(rem(x + dx, NX), z, c), v
        ).start()
    settle(tables.at[0, pl.ds(1, NQ - 1)], tab_recv.at[0])
    for way, piece in parts(1):
        if piece == 2:
            ring(way, 1, piece).start()
    pack_slots(0)
    loads[3].wait()

    def local(n, l):
        return jnp.clip(near_s[n, l] - (me - 1) * LEAF, 0, 3 * LEAF - 1)

    def chunk(i):
        for copy in chunk_copies(i):
            copy.wait()
        slot = i % 2

        @pl.loop(0, CHUNK // 2)
        def _(j):
            sides = []
            for t in range(2):
                l = 2 * j + t
                spot = i * CHUNK + l
                left, right = [], []
                for n in range(0, NEAR, 2):
                    left.append(join_tiles(near[local(n, spot)], near[local(n + 1, spot)]))
                    right.append(side(near_raw[slot, l, n], near_raw[slot, l, n + 1]))
                sides.append(dot_nt(jnp.concatenate(left, axis=1), jnp.concatenate(right, axis=1)))
                for e in range(FL):
                    block = leaf_raw[slot, l, e]
                    weights[i * CHUNK + l, :, pl.ds(e * 128, 128)] = diag(block, block)
            near_pair[i * (CHUNK // 2) + j] = side(*sides)

        if i + 2 < LEAF // CHUNK:
            for copy in chunk_copies(i + 2):
                copy.start()

    for step in range(1, NZ // 2 + 1):
        for way, piece in parts(step):
            ring(way, step, piece).wait_recv()
            if step < NZ // 2 and (way, piece) in parts(step + 1):
                ring(way, step + 1, piece).start()
        offs = (NZ - step, step) if step < NZ // 2 else (step,)
        for off in offs:
            pack_slots(off)
        box_step(step - 1)
        if step == 1:
            for copy in near_copies:
                copy.wait_recv()
        if step < NZ // 2:
            chunk(step - 1)

    for k in range(1, NX * NC):
        dx, dc = k // NC, k % NC
        remote(
            compact, rows_in.at[c * NX + x], rows_send, rows_recv,
            row(rem(x + dx, NX), z, rem(c + dc, NC)), v,
        ).start()
    rows_in[c * NX + x] = compact[...]
    chunk(3)
    box_step(NZ // 2)

    loads[5].wait()
    levels = (me // 4, NROWS // 4 + me // 2, 3 * NROWS // 4 + me)
    line = lax.broadcasted_iota(I32, (8, 112), 0)
    node = lax.broadcasted_iota(I32, (8, 112), 1)
    chosen = jnp.zeros((8, 112), F32)
    for i, n in enumerate(levels):
        chosen = jnp.where((line == i) & (node == n), 1.0, chosen)
    chosen = chosen.astype(BF)

    @pl.loop(0, 64)
    def _(r):
        for e in range(2):
            picked[e, r] = dot_nt(chosen, coupling_raw[e, r])

    for i in range(3):
        shared[0, 16 + i] = side(picked[0, :, i, :], picked[1, :, i, :]).astype(BF)
    for step in range(1, NQ):
        remote(
            shared.at[0, pl.ds(16, 3)], shared.at[NQ - step, pl.ds(16, 3)],
            shared_send.at[1], shared_recv.at[1], me, rem(v + step, NQ),
        ).start()

    loads[6].wait()
    same = lax.broadcasted_iota(I32, (96, 96), 0) == lax.broadcasted_iota(I32, (96, 96), 1)
    eye = jnp.where(same, 1.0, 0.0).astype(BF)

    @pl.loop(0, 64)
    def _(r):
        coarse[r] = dot_nt(eye, coarse_raw[r])

    loads[7].wait()
    settle(staged.at[pl.ds(1, GROUP - 1)], out_recv)
    settle(staged.at[0], self_sem)

    @pl.loop(0, BOX)
    def _(k):
        for i in range(8):
            l = k * 8 + i
            left = []
            for e in range(FL):
                entry = leaf_s[e, l]
                left.append(recv[:, entry // SLOTS, rem(entry, SLOTS)].reshape(64, 128))
            field = dot_nt(jnp.concatenate(left, axis=1), weights[l])
            part[:, l] = field.astype(BF).reshape(NQ, 16, 128)
        for step in range(1, NQ):
            q = rem(v + step, NQ)
            span = pl.ds(pl.multiple_of(k * 8, 8), 8)
            remote(
                part.at[q, span], arrived.at[step - 1, span], part_send, part_recv.at[k], me, q
            ).start()

    settle(lists.at[pl.ds(1, NQ - 1)], tab_recv.at[1])
    settle(shared.at[pl.ds(1, NQ - 1), pl.ds(0, 16)], shared_recv.at[0])
    settle(shared.at[pl.ds(1, NQ - 1), pl.ds(16, 3)], shared_recv.at[1])
    settle(rows_in.at[pl.ds(0, NX * NC - 1)], rows_recv)
    for q in range(NQ):
        lists_v[pl.ds(8 * q, 8), :] = lists[q]
    column = (x * NC + c) * 16 + SLOTS
    for i in range(2):
        block = rows_in[pl.ds(4 * i, 4)].reshape(128, 128)
        turned = pltpu.roll(block, rem(128 - column, 128), 1)
        rows_v[:, i * 128 : (i + 1) * 128] = jnp.transpose(turned)[:8]
    fetches = [
        pltpu.make_async_copy(lists_v, lists_s, load.at[0]),
        pltpu.make_async_copy(rows_v, rows_s, load.at[1]),
    ]
    for fetch in fetches:
        fetch.start()
    settle(every.at[pl.ds(0, NX * NZ)], sibling_recv)
    for fetch in fetches:
        fetch.wait()

    def matrix(n):
        return coarse[:, n, :].astype(BF)

    def place_of(p):
        return block_of(rem(p, NC), rem(p // NC, NZ)) + p // (NC * NZ)

    @pl.loop(0, NROWS // 2)
    def _(n):
        pair = join_tiles(every[place_of(2 * n), BOX], every[place_of(2 * n + 1), BOX])
        pile = jnp.concatenate([matrix(32 + 2 * n), matrix(33 + 2 * n)], axis=0)
        upper[16 + n] = dot_nn(pair, pile).astype(BF)

    @pl.loop(0, NROWS // 4)
    def _(n):
        pair = side(upper[16 + 2 * n], upper[17 + 2 * n])
        pile = jnp.concatenate([matrix(2 * n), matrix(2 * n + 1)], axis=0)
        upper[n] = dot_nn(pair, pile).astype(BF)

    field = jnp.zeros((32, 64), F32)
    for level in range(3):
        if level == 1:
            field = dot_nt(field.astype(BF), matrix(me // 2))
        if level == 2:
            field = dot_nt(field.astype(BF), matrix(32 + me))
        for q in range(NQ):
            a, b = (lists_s[8 * q + FB + e, levels[level]] for e in range(2))
            if level < 2:
                pair = side(upper[a], upper[b])
            else:
                pair = join_tiles(every[place_of(jnp.maximum(a - 48, 0)), BOX], every[place_of(jnp.maximum(b - 48, 0)), BOX])
            field += dot_nt(pair, shared[q, 16 + level])
    root = field.astype(BF)

    @pl.loop(0, BOX)
    def _(k):
        left, right = [], []
        for q in range(NQ):
            for m in range(FB // 2):
                tiles = []
                for e in range(2):
                    entry = lists_s[8 * q + 2 * m + e, k]
                    p = entry // 2
                    source = rem(p, NC) * NX + p // (NC * NZ)
                    zz = rem(p // NC, NZ)
                    number = rows_s[rem(entry, 2), (source * NZ + zz) * NQ + q]
                    tiles.append(every[place_of(p), jnp.maximum(number, 0)])
                left.append(join_tiles(*tiles))
                right.append(shared[q, 2 * k + m])
        box = dot_nt(root, box_transfer[k])
        box += dot_nt(jnp.concatenate(left, axis=1), jnp.concatenate(right, axis=1))
        wide = dot_nt(box.astype(BF), leaf_transfer[pl.ds(k * 8, 8)].reshape(512, 64))
        for j in range(4):
            base_pair[4 * k + j] = wide[:, j * 128 : (j + 1) * 128]

    @pl.loop(0, BOX)
    def _(k):
        span = pl.ds(pl.multiple_of(k * 8, 8), 8)
        settle(arrived.at[:, span], part_recv.at[k])
        for i in range(4):
            j = 4 * k + i
            fields = []
            for t in range(2):
                field = part[v, 2 * j + t].astype(F32)
                for step in range(NQ - 1):
                    field += arrived[step, 2 * j + t].astype(F32)
                fields.append(field)
            pair = (join_pair(*fields) + base_pair[j]).astype(BF)
            value = dot_nt(pair, basis_pair[j]) + near_pair[j]
            out[:, pl.ds(pl.multiple_of(j * 128, 128), 128)] = value.astype(BF)

    for step in range(1, NZ // 2 + 1):
        for way, piece in parts(step):
            ring(way, step, piece).wait_send()
    settle(tables.at[0, pl.ds(1, NQ - 1)], tab_send.at[0])
    settle(lists.at[pl.ds(1, NQ - 1)], tab_send.at[1])
    settle(staged.at[pl.ds(1, GROUP - 1)], out_send)
    settle(every.at[pl.ds(0, NZ * NX + NX - 1)], every_send)
    for step in range(1, NZ // 2 + 1):
        for way in box_ways(step):
            box_ring(way, step).wait_send()
    settle(rows_in.at[pl.ds(0, NX * NC - 1)], rows_send)
    settle(shared.at[pl.ds(1, NQ - 1), pl.ds(0, 16)], shared_send.at[0])
    settle(shared.at[pl.ds(1, NQ - 1), pl.ds(16, 3)], shared_send.at[1])
    settle(arrived, part_send)
    for copy in near_copies:
        copy.wait_send()


def product(points, *arrays):
    vmem, hbm = pl.BlockSpec(memory_space=pltpu.VMEM), pl.BlockSpec(memory_space=pl.ANY)
    dma = pltpu.SemaphoreType.DMA
    return pl.pallas_call(
        kernel,
        out_shape=jax.ShapeDtypeStruct((32, LEAF * 64), BF),
        in_specs=[vmem] * 5 + [hbm] * 10,
        out_specs=vmem,
        scratch_shapes=[
            *[pltpu.VMEM((LEAF, 16, 128), BF)] * NZ,
            pltpu.VMEM((128, 128), I32),
            pltpu.VMEM((128, 128), I32),
            pltpu.VMEM((8, 128), I32),
            pltpu.VMEM((NZ, NQ, 8, 128), I32),
            pltpu.VMEM((NZ, NQ, 128), I32),
            pltpu.SMEM((NZ, NQ, 128), I32),
            pltpu.VMEM((NQ, 8, 128), I32),
            pltpu.VMEM((NQ * 8, 128), I32),
            pltpu.SMEM((NQ * 8, 128), I32),
            pltpu.SMEM((FL, LEAF), I32),
            pltpu.SMEM((NEAR, LEAF), I32),
            pltpu.VMEM((GROUP, NZ, SLOTS, 16, 128), BF),
            pltpu.VMEM((NQ, NROWS, SLOTS, 16, 128), BF),
            pltpu.VMEM((NROWS, TOP, 16, 128), BF),
            pltpu.VMEM((NX * NC, NZ, NQ, 128), I32),
            pltpu.VMEM((8, 256), I32),
            pltpu.SMEM((8, 256), I32),
            pltpu.VMEM((3 * LEAF, 16, 128), BF),
            pltpu.VMEM((LEAF // 2, 32, 128), F32),
            pltpu.VMEM((LEAF // 2, 32, 128), F32),
            pltpu.VMEM((LEAF // 2, 128, 128), BF),
            pltpu.VMEM((LEAF, 128, FL * 128), BF),
            pltpu.VMEM((LEAF, 64, 64), BF),
            pltpu.VMEM((LEAF, 64, 64), BF),
            pltpu.VMEM((BOX, 64, 64), BF),
            pltpu.VMEM((BOX, FB, 64, 64), BF),
            pltpu.VMEM((64, 64, 96), BF),
            pltpu.VMEM((2, 64, 64, 112), BF),
            pltpu.VMEM((2, CHUNK, NEAR, 64, 64), BF),
            pltpu.VMEM((2, CHUNK, FL, 64, 64), BF),
            pltpu.VMEM((64, 96, 64), F32),
            pltpu.VMEM((2, 64, 8, 64), F32),
            pltpu.VMEM((NQ, 19, 64, 128), BF),
            pltpu.VMEM((48, 32, 64), BF),
            pltpu.VMEM((NQ, LEAF, 16, 128), BF),
            pltpu.VMEM((NQ - 1, LEAF, 16, 128), BF),
            dma((8,)),
            dma((2, 2)),
            dma((2,)),
            dma((2,)),
            dma((2, NZ // 2, 3)),
            dma((NZ, 3)),
            dma,
            dma,
            dma,
            dma((2,)),
            dma((2,)),
            dma,
            dma,
            dma,
            dma,
            dma((2, NZ // 2)),
            dma((NZ,)),
            dma,
            dma,
            dma((2,)),
            dma((2,)),
            dma,
            dma((BOX,)),
        ],
        compiler_params=pltpu.CompilerParams(
            collective_id=0, has_side_effects=True, vmem_limit_bytes=60 * 2**20
        ),
        name="product",
    )(points, *arrays)


def body(
    points, basis, leaf_transfer, box_transfer, coarse_transfer, send_leaf, leaf_far, leaf_coupling,
    send_box, box_far, box_coupling, coarse_far, coarse_coupling, near_index, near_block,
):
    return product(
        points, send_leaf.T, send_box.T, box_far.T, coarse_far.T, leaf_far.T, near_index.T, basis, leaf_transfer, box_transfer,
        leaf_coupling, box_coupling, coarse_transfer.transpose(1, 2, 0),
        coarse_coupling.transpose(1, 2, 3, 0), near_block,
    )


def solution(mesh):
    return jax.shard_map(
        body,
        mesh=mesh,
        in_specs=(
            P("cols", "rows"),
            P("rows", None, None),
            P("rows", None, None),
            P("rows", None, None),
            P(),
            P("rows", "cols"),
            P("rows", "cols"),
            P("rows", "cols", None, None),
            P("rows", "cols"),
            P("rows", "cols"),
            P("rows", "cols", None, None),
            P(None, "cols"),
            P(None, "cols", None, None),
            P("rows", None),
            P("rows", None, None, None),
        ),
        out_specs=P("cols", "rows"),
        check_vma=False,
    )
```

```python
import jax
import jax.numpy as jnp
from jax import lax
from jax.experimental import pallas as pl
from jax.experimental.pallas import tpu as pltpu
from jax.sharding import PartitionSpec as P

BF = jnp.bfloat16
F32 = jnp.float32
I32 = jnp.int32
MESH = pl.DeviceIdType.MESH
NX, NZ, NC, NQ = 4, 8, 2, 4
NROWS = NX * NZ * NC
LEAF, BOX, NEAR = 64, 8, 8
FL, FB = 6, 4
TOP = BOX + 1
SLOTS = 4
GROUP = NX * NC * NQ
CHUNK = 16


def rem(a, n):
    return lax.rem(a, n)


def side(a, b):
    return jnp.concatenate([a, b], axis=1)


def diag(first, second):
    zero = jnp.zeros_like(first)
    return jnp.concatenate([side(first, zero), side(zero, second)], axis=0)


def dot_nn(a, b):
    return lax.dot_general(a, b, (((1,), (0,)), ((), ())), preferred_element_type=F32)


def dot_nt(a, b):
    return lax.dot_general(a, b, (((1,), (1,)), ((), ())), preferred_element_type=F32)


def split_pair(wide):
    low, high = wide[:16], wide[16:]
    low_turned, high_turned = pltpu.roll(low, 64, 1), pltpu.roll(high, 64, 1)
    first = lax.broadcasted_iota(I32, (16, 128), 1) < 64
    return jnp.where(first, low, high_turned), jnp.where(first, low_turned, high)


def join_pair(even, odd):
    even_turned, odd_turned = pltpu.roll(even, 64, 1), pltpu.roll(odd, 64, 1)
    first = lax.broadcasted_iota(I32, (16, 128), 1) < 64
    return jnp.concatenate(
        [jnp.where(first, even, odd_turned), jnp.where(first, even_turned, odd)], axis=0
    )


def join_tiles(even, odd):
    return join_pair(even.astype(F32), odd.astype(F32)).astype(BF)


def kernel(
    points, send_leaf, send_box, box_far, coarse_far, leaf_far, near_index, basis_h, leaf_h, box_h, leaf_coupling, box_coupling, coarse_h, coarse_coupling,
    near_block, out, *scratch,
):
    held, scratch = scratch[:NZ], scratch[NZ:]
    (
        raw, turned_raw, table, tables, compact, index, lists, lists_v, lists_s, leaf_s, near_s, staged, recv, every,
        rows_in, rows_v, rows_s,
        near, near_pair, base_pair, basis_pair, weights,
        basis, leaf_transfer, box_transfer, box_raw, coarse_raw, coupling_raw, near_raw, leaf_raw,
        coarse, piles, picked, shared, upper, part, arrived,
    ) = scratch[:37]
    (
        load, chunk_load, tab_send, tab_recv, ring_send, ring_recv, out_send, out_recv, self_sem,
        near_send, near_recv, index_sem, every_send, every_recv, sibling_recv, box_send, box_recv,
        rows_send, rows_recv, shared_send, shared_recv, part_send, part_recv,
    ) = scratch[37:]
    mine = held[0]
    me, v = lax.axis_index("rows"), lax.axis_index("cols")
    c = rem(me, NC)
    z = rem(me // NC, NZ)
    x = me // (NC * NZ)

    def row(xx, zz, cc):
        return (xx * NZ + zz) * NC + cc

    def target(k):
        dx, dc, dq = k // (NC * NQ), rem(k // NQ, NC), rem(k, NQ)
        return row(rem(x + dx, NX), z, rem(c + dc, NC)), rem(v + dq, NQ), dq

    def remote(src, dst, send, arrive, d, q):
        return pltpu.make_async_remote_copy(
            src_ref=src, dst_ref=dst, send_sem=send, recv_sem=arrive,
            device_id=(d, q), device_id_type=MESH,
        )

    def settle(ref, sem):
        pltpu.make_async_copy(ref, ref, sem).wait()

    loads = [
        pltpu.make_async_copy(src, dst, load.at[i])
        for i, (src, dst) in enumerate((
            (basis_h, basis), (leaf_h, leaf_transfer), (box_h, box_transfer),
            (near_index, near_s), (box_coupling, box_raw),
            (coarse_coupling, coupling_raw), (coarse_h, coarse_raw), (leaf_far, leaf_s),
        ))
    ]
    loads[0].start()

    def chunk_copies(i):
        part_of = pl.ds(i * CHUNK, CHUNK)
        return (
            pltpu.make_async_copy(near_block.at[part_of], near_raw.at[i % 2], chunk_load.at[0, i % 2]),
            pltpu.make_async_copy(leaf_coupling.at[part_of], leaf_raw.at[i % 2], chunk_load.at[1, i % 2]),
        )

    z_up, z_down = row(x, rem(z + 1, NZ), c), row(x, rem(z + NZ - 1, NZ), c)
    sibling = row(x, z, 1 - c)
    far_side = rem(me + 2 * c - 1 + NROWS, NROWS)
    barrier = pltpu.get_barrier_semaphore()

    @pl.loop(1, GROUP)
    def _(k):
        d, q, _ = target(k)
        pl.semaphore_signal(barrier, inc=1, device_id=(d, q), device_id_type=MESH)

    for d in (z_up, z_down, far_side):
        pl.semaphore_signal(barrier, inc=1, device_id=(d, v), device_id_type=MESH)
    raw[...] = jnp.zeros((128, 128), I32)
    raw[pl.ds(0, SLOTS), pl.ds(0, NROWS)] = send_leaf[...]
    raw[pl.ds(SLOTS, 2), pl.ds(0, NROWS)] = send_box[...]
    turned_raw[...] = jnp.transpose(raw[...])
    lane = lax.broadcasted_iota(I32, (8, 128), 1)
    rows = jnp.zeros((8, 128), I32)
    for i in range(NX):
        for j in range(NC):
            column = i * 32 + j * 16
            lines = turned_raw[pl.ds(i * NZ * NC + j, NZ, stride=NC), :]
            rows = jnp.where((lane >= column) & (lane < column + 16), pltpu.roll(lines, column, 1), rows)
    table[...] = rows
    tables[0, 0] = rows
    lists[0] = jnp.zeros((8, 128), I32)
    lists[0, pl.ds(0, FB), pl.ds(0, BOX)] = box_far[...]
    lists[0, pl.ds(FB, 2), pl.ds(0, 112)] = coarse_far[...]

    @pl.loop(0, LEAF // 2)
    def _(j):
        block = points[:, pl.ds(pl.multiple_of(j * 128, 128), 128)]
        even, odd = split_pair(block.astype(F32))
        near[LEAF + 2 * j] = even.astype(BF)
        near[LEAF + 2 * j + 1] = odd.astype(BF)

    loads[0].wait()
    for copy in loads[1:]:
        copy.start()
    for i in range(2):
        for copy in chunk_copies(i):
            copy.start()

    def coefficients(k):
        for j in range(4):
            pair = k * 4 + j
            block = points[:, pl.ds(pl.multiple_of(pair * 128, 128), 128)]
            wide = diag(basis[2 * pair], basis[2 * pair + 1])
            basis_pair[pair] = wide
            coef = dot_nn(block, wide)
            near_pair[pair] = coef
            even, odd = split_pair(coef)
            mine[2 * pair] = even.astype(BF)
            mine[2 * pair + 1] = odd.astype(BF)

    pl.loop(0, BOX)(coefficients)

    pl.semaphore_wait(barrier, GROUP + 2)

    for step in range(1, NQ):
        q = rem(v + step, NQ)
        remote(table, tables.at[0, NQ - step], tab_send.at[0], tab_recv.at[0], me, q).start()
        remote(lists.at[0], lists.at[NQ - step], tab_send.at[1], tab_recv.at[1], me, q).start()
    own_near = near.at[pl.ds(LEAF, LEAF)]
    near_copies = (
        remote(own_near, near.at[pl.ds(0, LEAF)], near_send.at[0], near_recv.at[0], rem(me + 1, NROWS), v),
        remote(own_near, near.at[pl.ds(2 * LEAF, LEAF)], near_send.at[1], near_recv.at[1], rem(me + NROWS - 1, NROWS), v),
    )

    PIECES = {0: pl.ds(0, 32), 1: pl.ds(32, 32)}

    def ring(way, step, piece):
        if way == 0:
            src, dst, to = (NZ - step + 1) % NZ, NZ - step, z_up
        else:
            src, dst, to = step - 1, step, z_down
        if piece == 2:
            src_ref, dst_ref = tables.at[src], tables.at[dst]
        else:
            src_ref, dst_ref = held[src].at[PIECES[piece]], held[dst].at[PIECES[piece]]
        return remote(
            src_ref, dst_ref, ring_send.at[way, step - 1, piece], ring_recv.at[dst, piece], to, v
        )

    def parts(step):
        if step < NZ // 2:
            return [(way, piece) for piece in (2, 0, 1) for way in (0, 1)]
        return [(0, 2), (0, 0), (1, 1)]

    for way, piece in parts(1):
        if piece != 2:
            ring(way, 1, piece).start()
    for copy in near_copies:
        copy.start()

    def box_coefficients(k):
        wide = jnp.concatenate([near_pair[4 * k + j].astype(BF) for j in range(4)], axis=1)
        box = dot_nn(wide, leaf_transfer[pl.ds(k * 8, 8)].reshape(512, 64))
        every[place, k] = side(box[:16], box[16:]).astype(BF)

    def read_rows(off):
        for q in range(NQ):
            compact[rem(z + off, NZ), pl.ds(q, 1), :] = tables[off, q, pl.ds(z, 1), :]

    def pack_slots(off):
        fetch = pltpu.make_async_copy(compact.at[rem(z + off, NZ)], index.at[off], index_sem)
        fetch.start()
        fetch.wait()
        source = row(x, rem(z + off, NZ), c)

        def fill(k):
            d, q, dq = target(k)
            lo = rem(x + k // (NC * NQ), NX) * 32 + rem(c + rem(k // NQ, NC), NC) * 16
            for j in range(SLOTS):
                tile = jnp.maximum(index[off, dq, lo + j], 0)
                staged[k, off, j] = held[off][tile]
            return d, q

        @pl.loop(1, GROUP)
        def _(k):
            d, q = fill(k)
            remote(staged.at[k, off], recv.at[v, source], out_send, out_recv, d, q).start()

        fill(0)
        pltpu.make_async_copy(staged.at[0, off], recv.at[v, source], self_sem).start()

    def block_of(cc, zz):
        return (cc * NZ + zz) * NX

    place = block_of(c, z) + x

    def box_ring(way, step):
        src = (NZ - step + 1) % NZ if way == 0 else step - 1
        dst = NZ - step if way == 0 else step
        block = every.at[pl.ds(block_of(c, rem(z + src, NZ)), NX)]
        return remote(
            block, block, box_send.at[way, step - 1], box_recv.at[dst], (z_up, z_down)[way], v
        )

    def box_ways(step):
        return (0, 1) if step < NZ // 2 else (0,)

    def box_step(step):
        if step == 0:
            settle(every.at[pl.ds(0, NX - 1)], every_recv)
        else:
            for way in box_ways(step):
                box_ring(way, step).wait_recv()
        if step < NZ // 2:
            for way in box_ways(step + 1):
                box_ring(way, step + 1).start()
        for off in {0: (0,), NZ // 2: (NZ // 2,)}.get(step, (NZ - step, step)):
            block = every.at[pl.ds(block_of(c, rem(z + off, NZ)), NX)]
            remote(block, block, every_send, sibling_recv, sibling, v).start()

    loads[4].wait()

    @pl.loop(0, BOX)
    def _(k):
        for m in range(2):
            shared[0, 2 * k + m] = side(box_raw[k, 2 * m], box_raw[k, 2 * m + 1])

    def share(way, hop):
        step = 1 if way == 0 else NQ - 1
        span = pl.ds(0, 16) if hop == 0 else pl.ds(8 * way, 8)
        source, place_there = (0, NQ - step) if hop == 0 else (NQ - step, 2)
        return remote(
            shared.at[source, span], shared.at[place_there, span],
            shared_send.at[1 + 2 * hop + way], shared_recv.at[1 + 2 * hop + way],
            me, rem(v + step, NQ),
        )

    for way in range(2):
        share(way, 0).start()
    loads[1].wait()
    loads[2].wait()
    pl.loop(0, BOX)(box_coefficients)
    total = jnp.zeros((32, 64), F32)
    for k in range(0, BOX, 2):
        pair = join_tiles(every[place, k], every[place, k + 1])
        total += dot_nn(pair, box_transfer[pl.ds(k, 2)].reshape(128, 64))
    every[place, BOX] = side(total[:16], total[16:]).astype(BF)
    for dx in range(1, NX):
        remote(
            every.at[place], every.at[place], every_send, every_recv, row(rem(x + dx, NX), z, c), v
        ).start()
    settle(tables.at[0, pl.ds(1, NQ - 1)], tab_recv.at[0])
    for way, piece in parts(1):
        if piece == 2:
            ring(way, 1, piece).start()
    read_rows(0)
    pack_slots(0)
    box_step(0)
    loads[5].wait()
    levels = (me // 4, NROWS // 4 + me // 2, 3 * NROWS // 4 + me)
    line = lax.broadcasted_iota(I32, (8, 112), 0)
    node = lax.broadcasted_iota(I32, (8, 112), 1)
    chosen = jnp.zeros((8, 112), F32)
    for i, n in enumerate(levels):
        chosen = jnp.where((line == i) & (node == n), 1.0, chosen)
    chosen = chosen.astype(BF)

    @pl.loop(0, 64)
    def _(r):
        for e in range(2):
            picked[e, r] = dot_nt(chosen, coupling_raw[e, r])

    for i in range(3):
        shared[0, 16 + i] = side(picked[0, :, i, :], picked[1, :, i, :]).astype(BF)
    for step in range(1, NQ):
        remote(
            shared.at[0, pl.ds(16, 3)], shared.at[NQ - step, pl.ds(16, 3)],
            shared_send.at[0], shared_recv.at[0], me, rem(v + step, NQ),
        ).start()

    loads[3].wait()

    def local(n, l):
        return jnp.clip(near_s[n, l] - (me - 1) * LEAF, 0, 3 * LEAF - 1)

    def chunk(i):
        for copy in chunk_copies(i):
            copy.wait()
        slot = i % 2

        @pl.loop(0, CHUNK // 2)
        def _(j):
            sides = []
            for t in range(2):
                l = 2 * j + t
                spot = i * CHUNK + l
                left, right = [], []
                for n in range(0, NEAR, 2):
                    left.append(join_tiles(near[local(n, spot)], near[local(n + 1, spot)]))
                    right.append(side(near_raw[slot, l, n], near_raw[slot, l, n + 1]))
                sides.append(dot_nt(jnp.concatenate(left, axis=1), jnp.concatenate(right, axis=1)))
                for e in range(FL):
                    block = leaf_raw[slot, l, e]
                    weights[i * CHUNK + l, :, pl.ds(e * 128, 128)] = diag(block, block)
            near_pair[i * (CHUNK // 2) + j] = side(*sides)

        if i + 2 < LEAF // CHUNK:
            for copy in chunk_copies(i + 2):
                copy.start()

    for step in range(1, NZ // 2 + 1):
        for way, piece in parts(step):
            ring(way, step, piece).wait_recv()
            if step < NZ // 2 and (way, piece) in parts(step + 1):
                ring(way, step + 1, piece).start()
        offs = (NZ - step, step) if step < NZ // 2 else (step,)
        for off in offs:
            read_rows(off)
        box_step(step)
        if step == NZ // 2:
            for k in range(1, NX * NC):
                dx, dc = k // NC, k % NC
                remote(
                    compact, rows_in.at[c * NX + x], rows_send, rows_recv,
                    row(rem(x + dx, NX), z, rem(c + dc, NC)), v,
                ).start()
            rows_in[c * NX + x] = compact[...]
        for off in offs:
            pack_slots(off)
        if step == 1:
            for way in range(2):
                share(way, 0).wait_recv()
                share(way, 1).start()
        if step == 1:
            for copy in near_copies:
                copy.wait_recv()
        if step < NZ // 2:
            chunk(step - 1)

    chunk(3)

    loads[6].wait()
    same = lax.broadcasted_iota(I32, (96, 96), 0) == lax.broadcasted_iota(I32, (96, 96), 1)
    eye = jnp.where(same, 1.0, 0.0).astype(BF)

    @pl.loop(0, 64)
    def _(r):
        coarse[r] = dot_nt(eye, coarse_raw[r])

    def matrix(n):
        return coarse[:, n, :].astype(BF)

    @pl.loop(0, 48)
    def _(n):
        piles[n] = jnp.concatenate([matrix(2 * n), matrix(2 * n + 1)], axis=0)

    loads[7].wait()
    settle(staged.at[pl.ds(1, GROUP - 1)], out_recv)
    settle(staged.at[0], self_sem)

    @pl.loop(0, BOX)
    def _(k):
        for i in range(8):
            l = k * 8 + i
            left = []
            for e in range(FL):
                entry = leaf_s[e, l]
                left.append(recv[:, entry // SLOTS, rem(entry, SLOTS)].reshape(64, 128))
            field = dot_nt(jnp.concatenate(left, axis=1), weights[l])
            part[:, l] = field.astype(BF).reshape(NQ, 16, 128)
        for step in range(1, NQ):
            q = rem(v + step, NQ)
            span = pl.ds(pl.multiple_of(k * 8, 8), 8)
            remote(
                part.at[q, span], arrived.at[step - 1, span], part_send, part_recv.at[k], me, q
            ).start()

    settle(lists.at[pl.ds(1, NQ - 1)], tab_recv.at[1])
    for way in range(2):
        share(way, 1).wait_recv()
    settle(shared.at[pl.ds(1, NQ - 1), pl.ds(16, 3)], shared_recv.at[0])
    settle(rows_in.at[pl.ds(0, NX * NC - 1)], rows_recv)
    for q in range(NQ):
        lists_v[pl.ds(8 * q, 8), :] = lists[q]
    column = (x * NC + c) * 16 + SLOTS
    for i in range(2):
        block = rows_in[pl.ds(4 * i, 4)].reshape(128, 128)
        turned = pltpu.roll(block, rem(128 - column, 128), 1)
        rows_v[:, i * 128 : (i + 1) * 128] = jnp.transpose(turned)[:8]
    fetches = [
        pltpu.make_async_copy(lists_v, lists_s, load.at[0]),
        pltpu.make_async_copy(rows_v, rows_s, load.at[1]),
    ]
    for fetch in fetches:
        fetch.start()
    settle(every.at[pl.ds(0, NX * NZ)], sibling_recv)
    for fetch in fetches:
        fetch.wait()

    def place_of(p):
        return block_of(rem(p, NC), rem(p // NC, NZ)) + p // (NC * NZ)

    @pl.loop(0, NROWS // 16)
    def _(m):
        for i in range(8):
            n = 8 * m + i
            pair = join_tiles(every[place_of(2 * n), BOX], every[place_of(2 * n + 1), BOX])
            upper[16 + n] = dot_nn(pair, piles[16 + n]).astype(BF)

    @pl.loop(0, NROWS // 32)
    def _(m):
        for i in range(8):
            n = 8 * m + i
            upper[n] = dot_nn(side(upper[16 + 2 * n], upper[17 + 2 * n]), piles[n]).astype(BF)

    field = jnp.zeros((32, 64), F32)
    for level in range(3):
        if level == 1:
            field = dot_nt(field.astype(BF), matrix(me // 2))
        if level == 2:
            field = dot_nt(field.astype(BF), matrix(32 + me))
        for q in range(NQ):
            a, b = (lists_s[8 * q + FB + e, levels[level]] for e in range(2))
            if level < 2:
                pair = side(upper[a], upper[b])
            else:
                pair = join_tiles(every[place_of(jnp.maximum(a - 48, 0)), BOX], every[place_of(jnp.maximum(b - 48, 0)), BOX])
            field += dot_nt(pair, shared[q, 16 + level])
    root = field.astype(BF)

    def box_field(k):
        left, right = [], []
        for q in range(NQ):
            for m in range(FB // 2):
                tiles = []
                for e in range(2):
                    entry = lists_s[8 * q + 2 * m + e, k]
                    p = entry // 2
                    source = rem(p, NC) * NX + p // (NC * NZ)
                    zz = rem(p // NC, NZ)
                    number = rows_s[rem(entry, 2), (source * NZ + zz) * NQ + q]
                    tiles.append(every[place_of(p), jnp.maximum(number, 0)])
                left.append(join_tiles(*tiles))
                right.append(shared[q, 2 * k + m])
        box = dot_nt(root, box_transfer[k])
        box += dot_nt(jnp.concatenate(left, axis=1), jnp.concatenate(right, axis=1))
        wide = dot_nt(box.astype(BF), leaf_transfer[pl.ds(k * 8, 8)].reshape(512, 64))
        for j in range(4):
            base_pair[4 * k + j] = wide[:, j * 128 : (j + 1) * 128]

    @pl.loop(0, 2)
    def _(m):
        for i in range(4):
            box_field(4 * m + i)

    @pl.loop(0, BOX)
    def _(k):
        span = pl.ds(pl.multiple_of(k * 8, 8), 8)
        settle(arrived.at[:, span], part_recv.at[k])
        for i in range(4):
            j = 4 * k + i
            fields = []
            for t in range(2):
                field = part[v, 2 * j + t].astype(F32)
                for step in range(NQ - 1):
                    field += arrived[step, 2 * j + t].astype(F32)
                fields.append(field)
            pair = (join_pair(*fields) + base_pair[j]).astype(BF)
            value = dot_nt(pair, basis_pair[j]) + near_pair[j]
            out[:, pl.ds(pl.multiple_of(j * 128, 128), 128)] = value.astype(BF)

    for step in range(1, NZ // 2 + 1):
        for way, piece in parts(step):
            ring(way, step, piece).wait_send()
    settle(tables.at[0, pl.ds(1, NQ - 1)], tab_send.at[0])
    settle(lists.at[pl.ds(1, NQ - 1)], tab_send.at[1])
    settle(staged.at[pl.ds(1, GROUP - 1)], out_send)
    settle(every.at[pl.ds(0, NZ * NX + NX - 1)], every_send)
    for step in range(1, NZ // 2 + 1):
        for way in box_ways(step):
            box_ring(way, step).wait_send()
    settle(rows_in.at[pl.ds(0, NX * NC - 1)], rows_send)
    for way in range(2):
        for hop in range(2):
            share(way, hop).wait_send()
    settle(shared.at[pl.ds(1, NQ - 1), pl.ds(16, 3)], shared_send.at[0])
    settle(arrived, part_send)
    for copy in near_copies:
        copy.wait_send()


def product(points, *arrays):
    vmem, hbm = pl.BlockSpec(memory_space=pltpu.VMEM), pl.BlockSpec(memory_space=pl.ANY)
    dma = pltpu.SemaphoreType.DMA
    return pl.pallas_call(
        kernel,
        out_shape=jax.ShapeDtypeStruct((32, LEAF * 64), BF),
        in_specs=[vmem] * 5 + [hbm] * 10,
        out_specs=vmem,
        scratch_shapes=[
            *[pltpu.VMEM((LEAF, 16, 128), BF)] * NZ,
            pltpu.VMEM((128, 128), I32),
            pltpu.VMEM((128, 128), I32),
            pltpu.VMEM((8, 128), I32),
            pltpu.VMEM((NZ, NQ, 8, 128), I32),
            pltpu.VMEM((NZ, NQ, 128), I32),
            pltpu.SMEM((NZ, NQ, 128), I32),
            pltpu.VMEM((NQ, 8, 128), I32),
            pltpu.VMEM((NQ * 8, 128), I32),
            pltpu.SMEM((NQ * 8, 128), I32),
            pltpu.SMEM((FL, LEAF), I32),
            pltpu.SMEM((NEAR, LEAF), I32),
            pltpu.VMEM((GROUP, NZ, SLOTS, 16, 128), BF),
            pltpu.VMEM((NQ, NROWS, SLOTS, 16, 128), BF),
            pltpu.VMEM((NROWS, TOP, 16, 128), BF),
            pltpu.VMEM((NX * NC, NZ, NQ, 128), I32),
            pltpu.VMEM((8, 256), I32),
            pltpu.SMEM((8, 256), I32),
            pltpu.VMEM((3 * LEAF, 16, 128), BF),
            pltpu.VMEM((LEAF // 2, 32, 128), F32),
            pltpu.VMEM((LEAF // 2, 32, 128), F32),
            pltpu.VMEM((LEAF // 2, 128, 128), BF),
            pltpu.VMEM((LEAF, 128, FL * 128), BF),
            pltpu.VMEM((LEAF, 64, 64), BF),
            pltpu.VMEM((LEAF, 64, 64), BF),
            pltpu.VMEM((BOX, 64, 64), BF),
            pltpu.VMEM((BOX, FB, 64, 64), BF),
            pltpu.VMEM((64, 64, 96), BF),
            pltpu.VMEM((2, 64, 64, 112), BF),
            pltpu.VMEM((2, CHUNK, NEAR, 64, 64), BF),
            pltpu.VMEM((2, CHUNK, FL, 64, 64), BF),
            pltpu.VMEM((64, 96, 64), F32),
            pltpu.VMEM((48, 128, 64), BF),
            pltpu.VMEM((2, 64, 8, 64), F32),
            pltpu.VMEM((NQ, 19, 64, 128), BF),
            pltpu.VMEM((48, 32, 64), BF),
            pltpu.VMEM((NQ, LEAF, 16, 128), BF),
            pltpu.VMEM((NQ - 1, LEAF, 16, 128), BF),
            dma((8,)),
            dma((2, 2)),
            dma((2,)),
            dma((2,)),
            dma((2, NZ // 2, 3)),
            dma((NZ, 3)),
            dma,
            dma,
            dma,
            dma((2,)),
            dma((2,)),
            dma,
            dma,
            dma,
            dma,
            dma((2, NZ // 2)),
            dma((NZ,)),
            dma,
            dma,
            dma((5,)),
            dma((5,)),
            dma,
            dma((BOX,)),
        ],
        compiler_params=pltpu.CompilerParams(
            collective_id=0, has_side_effects=True, vmem_limit_bytes=60 * 2**20
        ),
        name="product",
    )(points, *arrays)


def body(
    points, basis, leaf_transfer, box_transfer, coarse_transfer, send_leaf, leaf_far, leaf_coupling,
    send_box, box_far, box_coupling, coarse_far, coarse_coupling, near_index, near_block,
):
    return product(
        points, send_leaf.T, send_box.T, box_far.T, coarse_far.T, leaf_far.T, near_index.T, basis, leaf_transfer, box_transfer,
        leaf_coupling, box_coupling, coarse_transfer.transpose(1, 2, 0),
        coarse_coupling.transpose(1, 2, 3, 0), near_block,
    )


def solution(mesh):
    return jax.shard_map(
        body,
        mesh=mesh,
        in_specs=(
            P("cols", "rows"),
            P("rows", None, None),
            P("rows", None, None),
            P("rows", None, None),
            P(),
            P("rows", "cols"),
            P("rows", "cols"),
            P("rows", "cols", None, None),
            P("rows", "cols"),
            P("rows", "cols"),
            P("rows", "cols", None, None),
            P(None, "cols"),
            P(None, "cols", None, None),
            P("rows", None),
            P("rows", None, None, None),
        ),
        out_specs=P("cols", "rows"),
        check_vma=False,
    )
```

```python
import jax
import jax.numpy as jnp
from jax import lax
from jax.experimental import pallas as pl
from jax.experimental.pallas import tpu as pltpu
from jax.sharding import PartitionSpec as P

BF = jnp.bfloat16
F32 = jnp.float32
I32 = jnp.int32
MESH = pl.DeviceIdType.MESH
NX, NZ, NC, NQ = 4, 8, 2, 4
NROWS = NX * NZ * NC
LEAF, BOX, NEAR = 64, 8, 8
FL, FB = 6, 4
TOP = BOX + 1
SLOTS = 4
GROUP = NX * NC * NQ
CHUNK = 16


def rem(a, n):
    return lax.rem(a, n)


def side(a, b):
    return jnp.concatenate([a, b], axis=1)


def diag(first, second):
    zero = jnp.zeros_like(first)
    return jnp.concatenate([side(first, zero), side(zero, second)], axis=0)


def dot_nn(a, b):
    return lax.dot_general(a, b, (((1,), (0,)), ((), ())), preferred_element_type=F32)


def dot_nt(a, b):
    return lax.dot_general(a, b, (((1,), (1,)), ((), ())), preferred_element_type=F32)


def split_pair(wide):
    low, high = wide[:16], wide[16:]
    low_turned, high_turned = pltpu.roll(low, 64, 1), pltpu.roll(high, 64, 1)
    first = lax.broadcasted_iota(I32, (16, 128), 1) < 64
    return jnp.where(first, low, high_turned), jnp.where(first, low_turned, high)


def join_pair(even, odd):
    even_turned, odd_turned = pltpu.roll(even, 64, 1), pltpu.roll(odd, 64, 1)
    first = lax.broadcasted_iota(I32, (16, 128), 1) < 64
    return jnp.concatenate(
        [jnp.where(first, even, odd_turned), jnp.where(first, even_turned, odd)], axis=0
    )


def join_tiles(even, odd):
    return join_pair(even.astype(F32), odd.astype(F32)).astype(BF)


def kernel(
    points, send_leaf, send_box, box_far, coarse_far, leaf_far, near_index, basis_h, leaf_h, box_h, leaf_coupling, box_coupling, coarse_h, coarse_coupling,
    near_block, out, *scratch,
):
    held, scratch = scratch[:NZ], scratch[NZ:]
    (
        raw, turned_raw, table, tables, compact, index, lists, lists_v, lists_s, leaf_s, near_s, staged, recv, every,
        rows_in, rows_v, rows_s,
        near, near_pair, base_pair, basis_pair, weights,
        basis, leaf_transfer, box_transfer, box_raw, coarse_raw, coupling_raw, near_raw, leaf_raw,
        coarse, piles, picked, shared, upper, part, arrived,
    ) = scratch[:37]
    (
        load, chunk_load, tab_send, tab_recv, ring_send, ring_recv, out_send, out_recv, self_sem,
        near_send, near_recv, index_sem, every_send, every_recv, sibling_recv, box_send, box_recv,
        rows_send, rows_recv, shared_send, shared_recv, part_send, part_recv,
    ) = scratch[37:]
    mine = held[0]
    me, v = lax.axis_index("rows"), lax.axis_index("cols")
    c = rem(me, NC)
    z = rem(me // NC, NZ)
    x = me // (NC * NZ)

    def row(xx, zz, cc):
        return (xx * NZ + zz) * NC + cc

    def target(k):
        dx, dc, dq = rem(k, NX), k // (NX * NQ), rem(k + k // NX, NQ)
        return row(rem(x + dx, NX), z, rem(c + dc, NC)), rem(v + dq, NQ), dq

    def remote(src, dst, send, arrive, d, q):
        return pltpu.make_async_remote_copy(
            src_ref=src, dst_ref=dst, send_sem=send, recv_sem=arrive,
            device_id=(d, q), device_id_type=MESH,
        )

    def settle(ref, sem):
        pltpu.make_async_copy(ref, ref, sem).wait()

    loads = [
        pltpu.make_async_copy(src, dst, load.at[i])
        for i, (src, dst) in enumerate((
            (basis_h, basis), (leaf_h, leaf_transfer), (box_h, box_transfer),
            (near_index, near_s), (box_coupling, box_raw),
            (coarse_coupling, coupling_raw), (coarse_h, coarse_raw), (leaf_far, leaf_s),
        ))
    ]
    loads[0].start()

    def chunk_copies(i):
        part_of = pl.ds(i * CHUNK, CHUNK)
        return (
            pltpu.make_async_copy(near_block.at[part_of], near_raw.at[i % 2], chunk_load.at[0, i % 2]),
            pltpu.make_async_copy(leaf_coupling.at[part_of], leaf_raw.at[i % 2], chunk_load.at[1, i % 2]),
        )

    z_up, z_down = row(x, rem(z + 1, NZ), c), row(x, rem(z + NZ - 1, NZ), c)
    sibling = row(x, z, 1 - c)
    far_side = rem(me + 2 * c - 1 + NROWS, NROWS)
    barrier = pltpu.get_barrier_semaphore()

    @pl.loop(1, GROUP)
    def _(k):
        d, q, _ = target(k)
        pl.semaphore_signal(barrier, inc=1, device_id=(d, q), device_id_type=MESH)

    for d in (z_up, z_down, far_side):
        pl.semaphore_signal(barrier, inc=1, device_id=(d, v), device_id_type=MESH)
    raw[...] = jnp.zeros((128, 128), I32)
    raw[pl.ds(0, SLOTS), pl.ds(0, NROWS)] = send_leaf[...]
    raw[pl.ds(SLOTS, 2), pl.ds(0, NROWS)] = send_box[...]
    turned_raw[...] = jnp.transpose(raw[...])
    lane = lax.broadcasted_iota(I32, (8, 128), 1)
    rows = jnp.zeros((8, 128), I32)
    for i in range(NX):
        for j in range(NC):
            column = i * 32 + j * 16
            lines = turned_raw[pl.ds(i * NZ * NC + j, NZ, stride=NC), :]
            rows = jnp.where((lane >= column) & (lane < column + 16), pltpu.roll(lines, column, 1), rows)
    table[...] = rows
    tables[0, 0] = rows
    lists[0] = jnp.zeros((8, 128), I32)
    lists[0, pl.ds(0, FB), pl.ds(0, BOX)] = box_far[...]
    lists[0, pl.ds(FB, 2), pl.ds(0, 112)] = coarse_far[...]

    @pl.loop(0, LEAF // 2)
    def _(j):
        block = points[:, pl.ds(pl.multiple_of(j * 128, 128), 128)]
        even, odd = split_pair(block.astype(F32))
        near[LEAF + 2 * j] = even.astype(BF)
        near[LEAF + 2 * j + 1] = odd.astype(BF)

    loads[0].wait()
    for copy in loads[1:]:
        copy.start()
    for i in range(2):
        for copy in chunk_copies(i):
            copy.start()

    def coefficients(k):
        for j in range(4):
            pair = k * 4 + j
            block = points[:, pl.ds(pl.multiple_of(pair * 128, 128), 128)]
            wide = diag(basis[2 * pair], basis[2 * pair + 1])
            basis_pair[pair] = wide
            coef = dot_nn(block, wide)
            near_pair[pair] = coef
            even, odd = split_pair(coef)
            mine[2 * pair] = even.astype(BF)
            mine[2 * pair + 1] = odd.astype(BF)

    pl.loop(0, BOX)(coefficients)

    pl.semaphore_wait(barrier, GROUP + 2)

    for step in range(1, NQ):
        q = rem(v + step, NQ)
        remote(table, tables.at[0, NQ - step], tab_send.at[0], tab_recv.at[0], me, q).start()
        remote(lists.at[0], lists.at[NQ - step], tab_send.at[1], tab_recv.at[1], me, q).start()
    own_near = near.at[pl.ds(LEAF, LEAF)]
    near_copies = (
        remote(own_near, near.at[pl.ds(0, LEAF)], near_send.at[0], near_recv.at[0], rem(me + 1, NROWS), v),
        remote(own_near, near.at[pl.ds(2 * LEAF, LEAF)], near_send.at[1], near_recv.at[1], rem(me + NROWS - 1, NROWS), v),
    )

    PIECES = {0: pl.ds(0, 32), 1: pl.ds(32, 32)}

    def ring(way, step, piece):
        if way == 0:
            src, dst, to = (NZ - step + 1) % NZ, NZ - step, z_up
        else:
            src, dst, to = step - 1, step, z_down
        if piece == 2:
            src_ref, dst_ref = tables.at[src], tables.at[dst]
        else:
            src_ref, dst_ref = held[src].at[PIECES[piece]], held[dst].at[PIECES[piece]]
        return remote(
            src_ref, dst_ref, ring_send.at[way, step - 1, piece], ring_recv.at[dst, piece], to, v
        )

    def parts(step):
        if step < NZ // 2:
            return [(way, piece) for piece in (2, 0, 1) for way in (0, 1)]
        return [(0, 2), (0, 0), (1, 1)]

    for way, piece in parts(1):
        if piece != 2:
            ring(way, 1, piece).start()
    for copy in near_copies:
        copy.start()

    def box_coefficients(k):
        wide = jnp.concatenate([near_pair[4 * k + j].astype(BF) for j in range(4)], axis=1)
        box = dot_nn(wide, leaf_transfer[pl.ds(k * 8, 8)].reshape(512, 64))
        every[place, k] = side(box[:16], box[16:]).astype(BF)

    def read_rows(off):
        for q in range(NQ):
            compact[rem(z + off, NZ), pl.ds(q, 1), :] = tables[off, q, pl.ds(z, 1), :]

    def pack_slots(off):
        fetch = pltpu.make_async_copy(compact.at[rem(z + off, NZ)], index.at[off], index_sem)
        fetch.start()
        fetch.wait()
        source = row(x, rem(z + off, NZ), c)

        def fill(k):
            d, q, dq = target(k)
            lo = rem(x + rem(k, NX), NX) * 32 + rem(c + k // (NX * NQ), NC) * 16
            for j in range(SLOTS):
                tile = jnp.maximum(index[off, dq, lo + j], 0)
                staged[k, off, j] = held[off][tile]
            return d, q

        @pl.loop(1, GROUP)
        def _(k):
            d, q = fill(k)
            remote(staged.at[k, off], recv.at[v, source], out_send, out_recv, d, q).start()

        fill(0)
        pltpu.make_async_copy(staged.at[0, off], recv.at[v, source], self_sem).start()

    def block_of(cc, zz):
        return (cc * NZ + zz) * NX

    place = block_of(c, z) + x

    def box_ring(way, step):
        src = (NZ - step + 1) % NZ if way == 0 else step - 1
        dst = NZ - step if way == 0 else step
        block = every.at[pl.ds(block_of(c, rem(z + src, NZ)), NX)]
        return remote(
            block, block, box_send.at[way, step - 1], box_recv.at[dst], (z_up, z_down)[way], v
        )

    def box_ways(step):
        return (0, 1) if step < NZ // 2 else (0,)

    def box_step(step):
        if step == 0:
            settle(every.at[pl.ds(0, NX - 1)], every_recv)
        else:
            for way in box_ways(step):
                box_ring(way, step).wait_recv()
        if step < NZ // 2:
            for way in box_ways(step + 1):
                box_ring(way, step + 1).start()
        for off in {0: (0,), NZ // 2: (NZ // 2,)}.get(step, (NZ - step, step)):
            block = every.at[pl.ds(block_of(c, rem(z + off, NZ)), NX)]
            remote(block, block, every_send, sibling_recv, sibling, v).start()

    loads[1].wait()
    loads[2].wait()
    pl.loop(0, BOX)(box_coefficients)
    total = jnp.zeros((32, 64), F32)
    for k in range(0, BOX, 2):
        pair = join_tiles(every[place, k], every[place, k + 1])
        total += dot_nn(pair, box_transfer[pl.ds(k, 2)].reshape(128, 64))
    every[place, BOX] = side(total[:16], total[16:]).astype(BF)
    for dx in range(1, NX):
        remote(
            every.at[place], every.at[place], every_send, every_recv, row(rem(x + dx, NX), z, c), v
        ).start()
    loads[4].wait()

    @pl.loop(0, BOX)
    def _(k):
        for m in range(2):
            shared[0, 2 * k + m] = side(box_raw[k, 2 * m], box_raw[k, 2 * m + 1])

    def share(way, hop):
        step = 1 if way == 0 else NQ - 1
        span = pl.ds(0, 16) if hop == 0 else pl.ds(8 * way, 8)
        source, place_there = (0, NQ - step) if hop == 0 else (NQ - step, 2)
        return remote(
            shared.at[source, span], shared.at[place_there, span],
            shared_send.at[1 + 2 * hop + way], shared_recv.at[1 + 2 * hop + way],
            me, rem(v + step, NQ),
        )

    for way in range(2):
        share(way, 0).start()
    settle(tables.at[0, pl.ds(1, NQ - 1)], tab_recv.at[0])
    for way, piece in parts(1):
        if piece == 2:
            ring(way, 1, piece).start()
    read_rows(0)
    pack_slots(0)
    box_step(0)
    loads[5].wait()
    levels = (me // 4, NROWS // 4 + me // 2, 3 * NROWS // 4 + me)
    line = lax.broadcasted_iota(I32, (8, 112), 0)
    node = lax.broadcasted_iota(I32, (8, 112), 1)
    chosen = jnp.zeros((8, 112), F32)
    for i, n in enumerate(levels):
        chosen = jnp.where((line == i) & (node == n), 1.0, chosen)
    chosen = chosen.astype(BF)

    @pl.loop(0, 64)
    def _(r):
        for e in range(2):
            picked[e, r] = dot_nt(chosen, coupling_raw[e, r])

    for i in range(3):
        shared[0, 16 + i] = side(picked[0, :, i, :], picked[1, :, i, :]).astype(BF)
    for step in range(1, NQ):
        remote(
            shared.at[0, pl.ds(16, 3)], shared.at[NQ - step, pl.ds(16, 3)],
            shared_send.at[0], shared_recv.at[0], me, rem(v + step, NQ),
        ).start()

    loads[3].wait()

    def local(n, l):
        return jnp.clip(near_s[n, l] - (me - 1) * LEAF, 0, 3 * LEAF - 1)

    def chunk(i):
        for copy in chunk_copies(i):
            copy.wait()
        slot = i % 2

        @pl.loop(0, CHUNK // 2)
        def _(j):
            sides = []
            for t in range(2):
                l = 2 * j + t
                spot = i * CHUNK + l
                left, right = [], []
                for n in range(0, NEAR, 2):
                    left.append(join_tiles(near[local(n, spot)], near[local(n + 1, spot)]))
                    right.append(side(near_raw[slot, l, n], near_raw[slot, l, n + 1]))
                sides.append(dot_nt(jnp.concatenate(left, axis=1), jnp.concatenate(right, axis=1)))
                for e in range(FL):
                    block = leaf_raw[slot, l, e]
                    weights[i * CHUNK + l, :, pl.ds(e * 128, 128)] = diag(block, block)
            near_pair[i * (CHUNK // 2) + j] = side(*sides)

        if i + 2 < LEAF // CHUNK:
            for copy in chunk_copies(i + 2):
                copy.start()

    for step in range(1, NZ // 2 + 1):
        for way, piece in parts(step):
            ring(way, step, piece).wait_recv()
            if step < NZ // 2 and (way, piece) in parts(step + 1):
                ring(way, step + 1, piece).start()
        offs = (NZ - step, step) if step < NZ // 2 else (step,)
        for off in offs:
            read_rows(off)
        box_step(step)
        if step == NZ // 2:
            for k in range(1, NX * NC):
                dx, dc = k // NC, k % NC
                remote(
                    compact, rows_in.at[c * NX + x], rows_send, rows_recv,
                    row(rem(x + dx, NX), z, rem(c + dc, NC)), v,
                ).start()
            rows_in[c * NX + x] = compact[...]
        for off in offs:
            pack_slots(off)
        if step == 1:
            for way in range(2):
                share(way, 0).wait_recv()
                share(way, 1).start()
        if step == 1:
            for copy in near_copies:
                copy.wait_recv()
        if step < NZ // 2:
            chunk(step - 1)

    chunk(3)

    loads[6].wait()
    same = lax.broadcasted_iota(I32, (96, 96), 0) == lax.broadcasted_iota(I32, (96, 96), 1)
    eye = jnp.where(same, 1.0, 0.0).astype(BF)

    @pl.loop(0, 64)
    def _(r):
        coarse[r] = dot_nt(eye, coarse_raw[r])

    def matrix(n):
        return coarse[:, n, :].astype(BF)

    @pl.loop(0, 48)
    def _(n):
        piles[n] = jnp.concatenate([matrix(2 * n), matrix(2 * n + 1)], axis=0)

    loads[7].wait()
    settle(staged.at[pl.ds(1, GROUP - 1)], out_recv)
    settle(staged.at[0], self_sem)

    @pl.loop(0, BOX)
    def _(k):
        for i in range(8):
            l = k * 8 + i
            left = []
            for e in range(FL):
                entry = leaf_s[e, l]
                left.append(recv[:, entry // SLOTS, rem(entry, SLOTS)].reshape(64, 128))
            field = dot_nt(jnp.concatenate(left, axis=1), weights[l])
            part[:, l] = field.astype(BF).reshape(NQ, 16, 128)
        for step in range(1, NQ):
            q = rem(v + step, NQ)
            span = pl.ds(pl.multiple_of(k * 8, 8), 8)
            remote(
                part.at[q, span], arrived.at[step - 1, span], part_send, part_recv.at[k], me, q
            ).start()

    settle(lists.at[pl.ds(1, NQ - 1)], tab_recv.at[1])
    for way in range(2):
        share(way, 1).wait_recv()
    settle(shared.at[pl.ds(1, NQ - 1), pl.ds(16, 3)], shared_recv.at[0])
    settle(rows_in.at[pl.ds(0, NX * NC - 1)], rows_recv)
    for q in range(NQ):
        lists_v[pl.ds(8 * q, 8), :] = lists[q]
    column = (x * NC + c) * 16 + SLOTS
    for i in range(2):
        block = rows_in[pl.ds(4 * i, 4)].reshape(128, 128)
        turned = pltpu.roll(block, rem(128 - column, 128), 1)
        rows_v[:, i * 128 : (i + 1) * 128] = jnp.transpose(turned)[:8]
    fetches = [
        pltpu.make_async_copy(lists_v, lists_s, load.at[0]),
        pltpu.make_async_copy(rows_v, rows_s, load.at[1]),
    ]
    for fetch in fetches:
        fetch.start()
    settle(every.at[pl.ds(0, NX * NZ)], sibling_recv)
    for fetch in fetches:
        fetch.wait()

    def place_of(p):
        return block_of(rem(p, NC), rem(p // NC, NZ)) + p // (NC * NZ)

    @pl.loop(0, NROWS // 16)
    def _(m):
        for i in range(8):
            n = 8 * m + i
            pair = join_tiles(every[place_of(2 * n), BOX], every[place_of(2 * n + 1), BOX])
            upper[16 + n] = dot_nn(pair, piles[16 + n]).astype(BF)

    @pl.loop(0, NROWS // 32)
    def _(m):
        for i in range(8):
            n = 8 * m + i
            upper[n] = dot_nn(side(upper[16 + 2 * n], upper[17 + 2 * n]), piles[n]).astype(BF)

    field = jnp.zeros((32, 64), F32)
    for level in range(3):
        if level == 1:
            field = dot_nt(field.astype(BF), matrix(me // 2))
        if level == 2:
            field = dot_nt(field.astype(BF), matrix(32 + me))
        for q in range(NQ):
            a, b = (lists_s[8 * q + FB + e, levels[level]] for e in range(2))
            if level < 2:
                pair = side(upper[a], upper[b])
            else:
                pair = join_tiles(every[place_of(jnp.maximum(a - 48, 0)), BOX], every[place_of(jnp.maximum(b - 48, 0)), BOX])
            field += dot_nt(pair, shared[q, 16 + level])
    root = field.astype(BF)

    def box_field(k):
        left, right = [], []
        for q in range(NQ):
            for m in range(FB // 2):
                tiles = []
                for e in range(2):
                    entry = lists_s[8 * q + 2 * m + e, k]
                    p = entry // 2
                    source = rem(p, NC) * NX + p // (NC * NZ)
                    zz = rem(p // NC, NZ)
                    number = rows_s[rem(entry, 2), (source * NZ + zz) * NQ + q]
                    tiles.append(every[place_of(p), jnp.maximum(number, 0)])
                left.append(join_tiles(*tiles))
                right.append(shared[q, 2 * k + m])
        box = dot_nt(root, box_transfer[k])
        box += dot_nt(jnp.concatenate(left, axis=1), jnp.concatenate(right, axis=1))
        wide = dot_nt(box.astype(BF), leaf_transfer[pl.ds(k * 8, 8)].reshape(512, 64))
        for j in range(4):
            base_pair[4 * k + j] = wide[:, j * 128 : (j + 1) * 128]

    @pl.loop(0, 2)
    def _(m):
        for i in range(4):
            box_field(4 * m + i)

    @pl.loop(0, BOX)
    def _(k):
        span = pl.ds(pl.multiple_of(k * 8, 8), 8)
        settle(arrived.at[:, span], part_recv.at[k])
        for i in range(4):
            j = 4 * k + i
            fields = []
            for t in range(2):
                field = part[v, 2 * j + t].astype(F32)
                for step in range(NQ - 1):
                    field += arrived[step, 2 * j + t].astype(F32)
                fields.append(field)
            pair = (join_pair(*fields) + base_pair[j]).astype(BF)
            value = dot_nt(pair, basis_pair[j]) + near_pair[j]
            out[:, pl.ds(pl.multiple_of(j * 128, 128), 128)] = value.astype(BF)

    for step in range(1, NZ // 2 + 1):
        for way, piece in parts(step):
            ring(way, step, piece).wait_send()
    settle(tables.at[0, pl.ds(1, NQ - 1)], tab_send.at[0])
    settle(lists.at[pl.ds(1, NQ - 1)], tab_send.at[1])
    settle(staged.at[pl.ds(1, GROUP - 1)], out_send)
    settle(every.at[pl.ds(0, NZ * NX + NX - 1)], every_send)
    for step in range(1, NZ // 2 + 1):
        for way in box_ways(step):
            box_ring(way, step).wait_send()
    settle(rows_in.at[pl.ds(0, NX * NC - 1)], rows_send)
    for way in range(2):
        for hop in range(2):
            share(way, hop).wait_send()
    settle(shared.at[pl.ds(1, NQ - 1), pl.ds(16, 3)], shared_send.at[0])
    settle(arrived, part_send)
    for copy in near_copies:
        copy.wait_send()


def product(points, *arrays):
    vmem, hbm = pl.BlockSpec(memory_space=pltpu.VMEM), pl.BlockSpec(memory_space=pl.ANY)
    dma = pltpu.SemaphoreType.DMA
    return pl.pallas_call(
        kernel,
        out_shape=jax.ShapeDtypeStruct((32, LEAF * 64), BF),
        in_specs=[vmem] * 5 + [hbm] * 10,
        out_specs=vmem,
        scratch_shapes=[
            *[pltpu.VMEM((LEAF, 16, 128), BF)] * NZ,
            pltpu.VMEM((128, 128), I32),
            pltpu.VMEM((128, 128), I32),
            pltpu.VMEM((8, 128), I32),
            pltpu.VMEM((NZ, NQ, 8, 128), I32),
            pltpu.VMEM((NZ, NQ, 128), I32),
            pltpu.SMEM((NZ, NQ, 128), I32),
            pltpu.VMEM((NQ, 8, 128), I32),
            pltpu.VMEM((NQ * 8, 128), I32),
            pltpu.SMEM((NQ * 8, 128), I32),
            pltpu.SMEM((FL, LEAF), I32),
            pltpu.SMEM((NEAR, LEAF), I32),
            pltpu.VMEM((GROUP, NZ, SLOTS, 16, 128), BF),
            pltpu.VMEM((NQ, NROWS, SLOTS, 16, 128), BF),
            pltpu.VMEM((NROWS, TOP, 16, 128), BF),
            pltpu.VMEM((NX * NC, NZ, NQ, 128), I32),
            pltpu.VMEM((8, 256), I32),
            pltpu.SMEM((8, 256), I32),
            pltpu.VMEM((3 * LEAF, 16, 128), BF),
            pltpu.VMEM((LEAF // 2, 32, 128), F32),
            pltpu.VMEM((LEAF // 2, 32, 128), F32),
            pltpu.VMEM((LEAF // 2, 128, 128), BF),
            pltpu.VMEM((LEAF, 128, FL * 128), BF),
            pltpu.VMEM((LEAF, 64, 64), BF),
            pltpu.VMEM((LEAF, 64, 64), BF),
            pltpu.VMEM((BOX, 64, 64), BF),
            pltpu.VMEM((BOX, FB, 64, 64), BF),
            pltpu.VMEM((64, 64, 96), BF),
            pltpu.VMEM((2, 64, 64, 112), BF),
            pltpu.VMEM((2, CHUNK, NEAR, 64, 64), BF),
            pltpu.VMEM((2, CHUNK, FL, 64, 64), BF),
            pltpu.VMEM((64, 96, 64), F32),
            pltpu.VMEM((48, 128, 64), BF),
            pltpu.VMEM((2, 64, 8, 64), F32),
            pltpu.VMEM((NQ, 19, 64, 128), BF),
            pltpu.VMEM((48, 32, 64), BF),
            pltpu.VMEM((NQ, LEAF, 16, 128), BF),
            pltpu.VMEM((NQ - 1, LEAF, 16, 128), BF),
            dma((8,)),
            dma((2, 2)),
            dma((2,)),
            dma((2,)),
            dma((2, NZ // 2, 3)),
            dma((NZ, 3)),
            dma,
            dma,
            dma,
            dma((2,)),
            dma((2,)),
            dma,
            dma,
            dma,
            dma,
            dma((2, NZ // 2)),
            dma((NZ,)),
            dma,
            dma,
            dma((5,)),
            dma((5,)),
            dma,
            dma((BOX,)),
        ],
        compiler_params=pltpu.CompilerParams(
            collective_id=0, has_side_effects=True, vmem_limit_bytes=60 * 2**20
        ),
        name="product",
    )(points, *arrays)


def body(
    points, basis, leaf_transfer, box_transfer, coarse_transfer, send_leaf, leaf_far, leaf_coupling,
    send_box, box_far, box_coupling, coarse_far, coarse_coupling, near_index, near_block,
):
    return product(
        points, send_leaf.T, send_box.T, box_far.T, coarse_far.T, leaf_far.T, near_index.T, basis, leaf_transfer, box_transfer,
        leaf_coupling, box_coupling, coarse_transfer.transpose(1, 2, 0),
        coarse_coupling.transpose(1, 2, 3, 0), near_block,
    )


def solution(mesh):
    return jax.shard_map(
        body,
        mesh=mesh,
        in_specs=(
            P("cols", "rows"),
            P("rows", None, None),
            P("rows", None, None),
            P("rows", None, None),
            P(),
            P("rows", "cols"),
            P("rows", "cols"),
            P("rows", "cols", None, None),
            P("rows", "cols"),
            P("rows", "cols"),
            P("rows", "cols", None, None),
            P(None, "cols"),
            P(None, "cols", None, None),
            P("rows", None),
            P("rows", None, None, None),
        ),
        out_specs=P("cols", "rows"),
        check_vma=False,
    )
```
